32 devices in a mesh: groups: 2 (over x), worker: 2 (over core), tensor: 8 (over z, y).
Axes of the slice: x: 2, y: 2, z: 4, core: 2. Of those that a mesh axis runs over, the one named last changes fastest.
Arguments:
- tokens: bfloat16 [1024, 8192], P(('groups', 'worker'), 'tensor'), parts along dimension 0, may hold values from -6 to 6
- norm_gain: float32 [8192], replicated, may hold values from 0.5 to 1.5
- query_weight: bfloat16 [8192, 8192], P(None, 'tensor'), may hold values from -0.0625 to 0.0625
- key_weight: bfloat16 [8192, 1024], P(None, 'tensor'), may hold values from -0.15625 to 0.15625
- value_weight: bfloat16 [8192, 1024], P(None, 'tensor'), may hold values from -0.0625 to 0.0625
- output_weight: bfloat16 [8192, 8192], P('tensor'), may hold values from -0.0625 to 0.0625
- cached_blocks: bfloat16 [8, 1024, 2, 1024], P(('groups', 'worker'), 'tensor'), parts along dimension 0
- cache_length: int32 [8], P('groups'), parts along dimension 0, may hold values from 256 to 1024, as said below
- block_table: int32 [8, 64], P('groups'), parts along dimension 0, may hold values from 0 to 63, each once within a row
- destination: int32 [8], P('groups'), parts along dimension 0, may hold values from 0 to 1, as said below
Outputs:
- attended: bfloat16 [4, 3, 128, 8192], P(('groups', 'worker'), None, None, 'tensor'), parts along dimension 0
The draws below stay inside these ranges and needn't reach their ends.
There are 2 independent parts, one for each index of `groups`. The reference program is written for one: setup_inputs(seed, part) draws one part's arguments, and reference() takes and returns one part's arrays. A program takes and returns all parts, laid end to end along the dimension named above; an argument that names none is the same for every part. Nothing has to cross between parts.
Inputs may be any that keep to these rules, and one draw needn't show every extreme that they name: Exactly 3 sequences have one destination, the others the other; which one is drawn. `cache_length`: some sequence has exactly 1024 cached tokens.
All inputs are finite; a program needn't handle non-finite values.
Results may differ from the reference program's by a relative error of at most 0.02.
The reference program's roundings to bfloat16 on the way count: a program that leaves them out, or rounds other values in their place, can miss the bound.
Values may be sent and summed in bfloat16 or wider, within the bound.
A program may use at most 128 MiB of HBM per device.

```python
import math
import jax
import jax.numpy as jnp
from jax import lax

D = 8192
H = 64
KVH = 8
HD = 128
NEW = 128
BLK = 16
SEQS = 4
CAP = 3
CTX = 1024
NBLK = 64
N_WORKER = 2


def draw_cached_blocks(key, part):
    first, second = jax.random.split(jax.random.fold_in(key, 11), 2)
    keys_part = jax.random.normal(first, (SEQS, CTX, 1, KVH * HD), jnp.float32)
    values_part = jax.random.normal(second, (SEQS, CTX, 1, KVH * HD), jnp.float32)
    return jnp.concatenate([keys_part, values_part], axis=2).astype(jnp.bfloat16)


def draw_cache_length(key, part):
    first, second = jax.random.split(jax.random.fold_in(key, 23))
    lengths = jax.random.randint(first, (SEQS,), CTX // 4, CTX + 1)
    chosen = jax.random.randint(second, (), 0, SEQS)
    return jnp.where(jnp.arange(SEQS) == chosen, CTX, lengths).astype(jnp.int32)


def draw_destination(key, part):
    first, second = jax.random.split(jax.random.fold_in(key, 37))
    busiest = jax.random.randint(first, (), 0, 2)
    order = jax.random.permutation(second, SEQS)
    return jnp.where(order < CAP, busiest, 1 - busiest).astype(jnp.int32)


def block_levels(own_key, dims, cuts, smallest, top_value):
    loudness, own = 1.0, jax.random.fold_in(own_key, 6)
    for position, blocks in cuts:
        steps = jnp.exp(jax.random.uniform(jax.random.fold_in(own, position), (blocks,), jnp.float32, smallest / len(cuts), top_value / len(cuts)))
        loudness = loudness * jnp.repeat(steps, dims[position] // blocks).reshape([-1 if axis == position else 1 for axis in range(len(dims))])
    return loudness


def noise(rng, extent, scale, bound, cuts=(), held_as=jnp.bfloat16):
    values = jax.random.normal(rng, extent, jnp.float32) * scale
    if len(cuts) > 0:
        values = block_levels(rng, extent, cuts, -0.22, 0.18) * values
    return jnp.clip(values, min=-bound, max=bound).astype(held_as)


def setup_inputs(seed: int = 0, part: int = 0) -> dict:
    arg_keys = jax.random.split(jax.random.key(seed), 11)
    part_keys = jax.random.split(jax.random.fold_in(arg_keys[10], part), 11)
    return {
        "tokens": noise(part_keys[0], (SEQS * NEW, D), 1.0, 6.0, ((0, 2), (1, 8))),
        "norm_gain": jnp.clip(1.0 + 0.1 * jax.random.normal(arg_keys[1], (D,), jnp.float32), 0.5, 1.5),
        "query_weight": noise(arg_keys[2], (D, H * HD), D ** -0.5, 0.0625, ((1, 8),)),
        "key_weight": noise(arg_keys[3], (D, KVH * HD), (D // 6) ** -0.5, 0.15625, ((1, 8),)),
        "value_weight": noise(arg_keys[4], (D, KVH * HD), D ** -0.5, 0.0625, ((1, 8),)),
        "output_weight": noise(arg_keys[5], (H * HD, D), (H * HD) ** -0.5, 0.0625, ((0, 8),)),
        "cached_blocks": draw_cached_blocks(jax.random.fold_in(jax.random.fold_in(arg_keys[10], part), 71), part),
        "cache_length": draw_cache_length(jax.random.fold_in(jax.random.fold_in(arg_keys[10], part), 71), part),
        "block_table": jax.vmap(lambda own: jax.random.permutation(own, NBLK))(jax.random.split(part_keys[8], SEQS)).reshape((SEQS, NBLK)).astype(jnp.int32),
        "destination": draw_destination(jax.random.fold_in(jax.random.fold_in(arg_keys[10], part), 71), part),
    }


epsilon = 1e-05

def rotate(values, positions):
    halfway = HD // 2
    inverse = 500000.0 ** (-(jnp.arange(halfway, dtype=jnp.float32) * 2.0 / HD))
    angles = positions[:, None] * inverse[None, :]
    cosine_table = jnp.concatenate([jnp.cos(angles), jnp.cos(angles)], axis=-1)[:, None, :]
    sine_table = jnp.concatenate([jnp.sin(angles), jnp.sin(angles)], axis=-1)[:, None, :]
    turned = jnp.concatenate([-values[..., halfway:], values[..., :halfway]], axis=-1)
    return values * cosine_table + turned * sine_table

def reference(tokens, norm_gain, query_weight, key_weight, value_weight, output_weight, cached_blocks, cache_length, block_table, destination):
    group_size = H // KVH

    def single(index):
        rows = lax.dynamic_slice_in_dim(tokens, index * NEW, NEW, 0).astype(jnp.float32)
        factor = lax.rsqrt(lax.optimization_barrier(jnp.mean(rows * rows, axis=1)) + epsilon)[:, None]
        scaled = (rows * norm_gain[None, :]).astype(jnp.bfloat16)
        positions = (cache_length[index] + jnp.arange(NEW, dtype=jnp.int32)).astype(jnp.float32)
        query = jnp.dot(scaled, query_weight, preferred_element_type=jnp.float32) * factor
        query = rotate(query.reshape(NEW, H, HD), positions).astype(jnp.bfloat16)
        key_raw = (jnp.dot(scaled, key_weight, preferred_element_type=jnp.float32) * factor).astype(jnp.bfloat16)
        key_raw = lax.optimization_barrier(key_raw)
        value = (jnp.dot(scaled, value_weight, preferred_element_type=jnp.float32) * factor).astype(jnp.bfloat16)
        key = rotate(key_raw.astype(jnp.float32).reshape(NEW, KVH, HD), positions).astype(jnp.bfloat16)
        value = value.reshape(NEW, KVH, HD)
        stored = lax.dynamic_index_in_dim(cached_blocks, index, 0, keepdims=False)
        old_key = stored[:, 0, :].reshape(CTX, KVH, HD)
        old_value = stored[:, 1, :].reshape(CTX, KVH, HD)
        slots = jnp.arange(CTX, dtype=jnp.int32)
        table_row = lax.dynamic_index_in_dim(block_table, index, 0, keepdims=False)
        logical = jnp.take(table_row, slots // BLK) * BLK + slots % BLK
        visible = logical < cache_length[index]
        causal = jnp.arange(NEW)[:, None] >= jnp.arange(NEW)[None, :]
        allowed = jnp.concatenate([jnp.broadcast_to(visible[None, :], (NEW, CTX)), causal], axis=1)
        all_keys = jnp.concatenate([old_key, key], axis=0).astype(jnp.float32)
        all_values = jnp.concatenate([old_value, value], axis=0).astype(jnp.float32)
        grouped = query.reshape(NEW, KVH, group_size, HD).astype(jnp.float32)
        scores = jnp.einsum('qhgd,khd->hgqk', grouped, all_keys) / math.sqrt(HD)
        scores = jnp.where(allowed[None, None], scores, -1e+30)
        largest = lax.optimization_barrier(jnp.max(scores, axis=3, keepdims=True))
        expo = jnp.exp(scores - largest)
        weights = (expo / lax.optimization_barrier(jnp.sum(expo, axis=3, keepdims=True))).astype(jnp.bfloat16)
        mixture = jnp.einsum('hgqk,khd->qhgd', weights.astype(jnp.float32), all_values)
        mixture = mixture.astype(jnp.bfloat16).reshape(NEW, H * HD)
        return jnp.dot(mixture, output_weight, preferred_element_type=jnp.float32).astype(jnp.bfloat16)
    finished = lax.map(single, jnp.arange(SEQS, dtype=jnp.int32))
    placed_all = []
    for worker_id in range(N_WORKER):
        belongs = (destination == worker_id).astype(jnp.int32)
        ranking = jnp.cumsum(belongs) - 1
        matched = (belongs[None, :] == 1) & (ranking[None, :] == jnp.arange(CAP, dtype=jnp.int32)[:, None])
        owner = lax.optimization_barrier(jnp.sum(matched.astype(jnp.int32) * jnp.arange(SEQS, dtype=jnp.int32)[None, :], axis=1))
        occupied = jnp.any(matched, axis=1)
        picked = jnp.take(finished, owner, axis=0)
        placed_all.append(jnp.where(occupied[:, None, None], picked, jnp.zeros_like(picked)))
    return jnp.stack(placed_all)
```

```python
import functools
import math

import jax
import jax.numpy as jnp
from jax import lax
from jax.experimental import pallas as pl
from jax.experimental.pallas import tpu as pltpu
from jax.sharding import PartitionSpec as P

HD = 128
NEW = 128
BLK = 16
CAP = 3
KVH = 8

MESH = pl.DeviceIdType.MESH
epsilon = 1e-05


def snake_order(count):
    def position(index):
        column, row = lax.rem(index, 2), lax.div(index, 2)
        return row + column * (count - 1 - 2 * row)

    def index(place):
        second = lax.div(place, count // 2)
        return second * (2 * (count - 1 - place) + 1) + (1 - second) * (2 * place)

    return position, index


def ring_order(mesh):
    devices = mesh.devices[0, 0]
    count = devices.shape[0]
    places = [getattr(device, "coords", None) for device in devices]
    if count > 2 and count % 2 == 0 and all(place is not None for place in places):
        ring = list(range(0, count, 2)) + list(range(count - 1, 0, -2))
        steps = [
            sum(abs(a - b) for a, b in zip(places[ring[k]], places[ring[(k + 1) % count]]))
            for k in range(count)
        ]
        if max(steps) == 1:
            return snake_order(count)
    return (lambda index: index), (lambda place: place)


def project_kernel(
    order, tok, gain, cosine, sine, wq, wk, wv, kvt,
    q_out, k_out, v_out, ctx,
    xg, wq_all, wk_all, wv_all, qacc, kacc, vacc, squares,
    weight_sem, send_sem, recv_sem, old_send, old_recv, own_sem,
):
    position, index = order
    n = xg.shape[0]
    half, part = xg.shape[3], xg.shape[4]
    width = 2 * part
    share = n // kvt.shape[0]
    me = lax.axis_index("tensor")
    place = position(me)
    forward = index(lax.rem(place + 1, n))
    back = index(lax.rem(place + n - 1, n))
    targets = (forward, back)
    streams = [(d, c) for c in range(2) for d in range(2)]

    def weight_copies(block):
        rows = pl.ds(pl.multiple_of(block * width, width), width)
        return [
            pltpu.make_async_copy(src.at[rows, :], dst.at[block], weight_sem.at[block, k])
            for k, (src, dst) in enumerate(((wq, wq_all), (wk, wk_all), (wv, wv_all)))
        ]

    def start_weights(k, carry):
        for copy in weight_copies(index(lax.rem(place + k, n))):
            copy.start()
        return carry

    def wait_weights(k, carry):
        for copy in weight_copies(index(lax.rem(place + k, n))):
            copy.wait()
        return carry

    barrier = pltpu.get_barrier_semaphore()

    def greet(k, carry):
        pl.semaphore_signal(
            barrier, inc=1, device_id={"tensor": lax.rem(me + k, n)}, device_id_type=MESH
        )
        return carry

    lax.fori_loop(1, n, greet, 0)
    lax.fori_loop(0, n, start_weights, 0)
    own = pltpu.make_async_copy(kvt.at[lax.div(me, share)], ctx.at[me], own_sem)
    own.start()
    for d, c in streams:
        xg[0, d, c] = tok[d * half : (d + 1) * half, c * part : (c + 1) * part]
    qacc[...] = jnp.zeros_like(qacc)
    kacc[...] = jnp.zeros_like(kacc)
    vacc[...] = jnp.zeros_like(vacc)
    squares[...] = jnp.zeros_like(squares)
    pl.semaphore_wait(barrier, n - 1)

    def hop(step, d, c):
        return pltpu.make_async_remote_copy(
            src_ref=xg.at[step, d, c],
            dst_ref=xg.at[step + 1, d, c],
            send_sem=send_sem.at[step, d, c],
            recv_sem=recv_sem.at[step + 1, d, c],
            device_id={"tensor": targets[d]},
            device_id_type=MESH,
        )

    def arrival(step, d, c):
        return pltpu.make_async_remote_copy(
            src_ref=xg.at[step, d, c],
            dst_ref=xg.at[step, d, c],
            send_sem=send_sem.at[step, d, c],
            recv_sem=recv_sem.at[step, d, c],
            device_id={"tensor": targets[d]},
            device_id_type=MESH,
        )

    def stored(k):
        target = lax.rem(me + k, n)
        return pltpu.make_async_remote_copy(
            src_ref=kvt.at[lax.div(target, share)],
            dst_ref=ctx.at[me],
            send_sem=old_send.at[k],
            recv_sem=old_recv.at[k],
            device_id={"tensor": target},
            device_id_type=MESH,
        )

    def stored_arrival(k):
        source = lax.rem(me + n - k, n)
        return pltpu.make_async_remote_copy(
            src_ref=kvt.at[0],
            dst_ref=ctx.at[source],
            send_sem=old_send.at[k],
            recv_sem=old_recv.at[k],
            device_id={"tensor": source},
            device_id_type=MESH,
        )

    def step_body(step, carry):
        blocks = (
            index(lax.rem(place + n - step, n)),
            index(lax.rem(place + step, n)),
        )
        for number, (d, c) in enumerate(streams):

            @pl.when(step > 0)
            def _():
                arrival(step, d, c).wait_recv()

            @pl.when(step < n - 1)
            def _():
                hop(step, d, c).start()

            if number == 0:

                @pl.when(step < n - 1)
                def _():
                    stored(step + 1).start()

                @pl.when(step == 0)
                def _():
                    wait_weights(0, 0)

                @pl.when(step == 1)
                def _():
                    lax.fori_loop(1, n, wait_weights, 0)

            block = blocks[d]
            values = xg[step, d, c].astype(jnp.float32)
            squares[d] += jnp.sum(values * values, axis=1, keepdims=True)
            offset = pl.multiple_of(block * width + c * part, part)
            scaled = (values * gain[:, pl.ds(offset, part)]).astype(jnp.bfloat16)
            rows = slice(c * part, (c + 1) * part)
            for total, weight in ((qacc, wq_all), (kacc, wk_all), (vacc, wv_all)):
                total[d] += jnp.dot(
                    scaled, weight[block, rows, :], preferred_element_type=jnp.float32
                )
        return carry

    lax.fori_loop(0, n, step_body, 0)

    for d in range(2):
        lines = slice(d * half, (d + 1) * half)
        factor = lax.rsqrt(squares[d] / (n * width) + epsilon)
        k_out[lines, :] = (kacc[d] * factor).astype(jnp.bfloat16)
        v_out[lines, :] = (vacc[d] * factor).astype(jnp.bfloat16)
        for head in range(q_out.shape[1] // HD):
            cols = slice(head * HD, (head + 1) * HD)
            query = qacc[d, :, cols] * factor
            turned = pltpu.roll(query, HD // 2, 1)
            q_out[lines, cols] = (query * cosine[lines, :] + turned * sine[lines, :]).astype(
                jnp.bfloat16
            )

    def finish(step, carry):
        for d, c in streams:
            hop(step, d, c).wait_send()
        stored(step + 1).wait_send()
        stored_arrival(step + 1).wait_recv()
        return carry

    lax.fori_loop(0, n - 1, finish, 0)
    own.wait()


def project(order, n, tokens, gain, cosine, sine, wq, wk, wv, kvt):
    rows, width = tokens.shape
    half, part = rows // 2, width // 2
    cols, narrow = wq.shape[1], wk.shape[1]
    vmem = pl.BlockSpec(memory_space=pltpu.VMEM)
    anywhere = pl.BlockSpec(memory_space=pl.ANY)
    return pl.pallas_call(
        functools.partial(project_kernel, order),
        out_shape=(
            jax.ShapeDtypeStruct((rows, cols), jnp.bfloat16),
            jax.ShapeDtypeStruct((rows, narrow), jnp.bfloat16),
            jax.ShapeDtypeStruct((rows, narrow), jnp.bfloat16),
            jax.ShapeDtypeStruct((n,) + kvt.shape[1:], jnp.bfloat16),
        ),
        in_specs=[vmem] * 4 + [anywhere] * 4,
        out_specs=(vmem, vmem, vmem, anywhere),
        scratch_shapes=[
            pltpu.VMEM((n, 2, 2, half, part), jnp.bfloat16),
            pltpu.VMEM((n, width, cols), jnp.bfloat16),
            pltpu.VMEM((n, width, narrow), jnp.bfloat16),
            pltpu.VMEM((n, width, narrow), jnp.bfloat16),
            pltpu.VMEM((2, half, cols), jnp.float32),
            pltpu.VMEM((2, half, narrow), jnp.float32),
            pltpu.VMEM((2, half, narrow), jnp.float32),
            pltpu.VMEM((2, half, 1), jnp.float32),
            pltpu.SemaphoreType.DMA((n, 3)),
            pltpu.SemaphoreType.DMA((n, 2, 2)),
            pltpu.SemaphoreType.DMA((n, 2, 2)),
            pltpu.SemaphoreType.DMA((n,)),
            pltpu.SemaphoreType.DMA((n,)),
            pltpu.SemaphoreType.DMA,
        ],
        compiler_params=pltpu.CompilerParams(
            collective_id=0, has_side_effects=True, vmem_limit_bytes=48 * 2**20
        ),
        name="gather_project",
    )(tokens, gain, cosine, sine, wq, wk, wv, kvt)


def attend_kernel(query, old, key_raw, value, cosine, sine, bias, mixture, key_turned):
    @pl.when(pl.program_id(1) == 0)
    def _():
        raw = key_raw[...].astype(jnp.float32)
        turned = pltpu.roll(raw, HD // 2, 1)
        key_turned[...] = (raw * cosine[...] + turned * sine[...]).astype(jnp.bfloat16)

    count = old.shape[0] * old.shape[3]
    old_key = old[:, 0, 0].reshape(count, HD)
    old_value = old[:, 0, 1].reshape(count, HD)
    inverse_root = 1.0 / math.sqrt(HD)
    across = (((1,), (1,)), ((), ()))
    old_scores = lax.dot_general(
        query[...], old_key, across, preferred_element_type=jnp.float32
    )
    new_scores = lax.dot_general(
        query[...], key_turned[...], across, preferred_element_type=jnp.float32
    )
    old_scores = jnp.where(bias[0] > 0, old_scores * inverse_root, -1e30)
    row = lax.broadcasted_iota(jnp.int32, new_scores.shape, 0)
    col = lax.broadcasted_iota(jnp.int32, new_scores.shape, 1)
    new_scores = jnp.where(row >= col, new_scores * inverse_root, -1e30)
    largest = jnp.maximum(
        jnp.max(old_scores, axis=1, keepdims=True), jnp.max(new_scores, axis=1, keepdims=True)
    )
    old_expo = jnp.exp(old_scores - largest)
    new_expo = jnp.exp(new_scores - largest)
    scale = 1.0 / (
        jnp.sum(old_expo, axis=1, keepdims=True) + jnp.sum(new_expo, axis=1, keepdims=True)
    )
    old_probs = (old_expo * scale).astype(jnp.bfloat16)
    new_probs = (new_expo * scale).astype(jnp.bfloat16)
    mixed = jnp.dot(old_probs, old_value, preferred_element_type=jnp.float32)
    mixed += jnp.dot(new_probs, value[...], preferred_element_type=jnp.float32)
    mixture[...] = mixed.astype(jnp.bfloat16)


def attention(query, old, key_raw, value, cosine, sine, bias):
    seqs = old.shape[1]
    heads = query.shape[1] // HD
    per_seq = pl.BlockSpec((NEW, HD), lambda s, h: (s, 0))
    per_head = pl.BlockSpec((NEW, HD), lambda s, h: (s, h))
    return pl.pallas_call(
        attend_kernel,
        out_shape=jax.ShapeDtypeStruct(query.shape, jnp.bfloat16),
        grid=(seqs, heads),
        in_specs=[
            per_head,
            pl.BlockSpec((old.shape[0], 1) + old.shape[2:], lambda s, h: (0, s, 0, 0, 0)),
            per_seq,
            per_seq,
            per_seq,
            per_seq,
            pl.BlockSpec((1, 1, bias.shape[2]), lambda s, h: (s, 0, 0)),
        ],
        out_specs=per_head,
        scratch_shapes=[pltpu.VMEM((NEW, HD), jnp.bfloat16)],
        compiler_params=pltpu.CompilerParams(vmem_limit_bytes=48 * 2**20),
        name="attention",
    )(query, old, key_raw, value, cosine, sine, bias)


def output_kernel(
    order, mixture, weight, everyone,
    weight_all, outgoing, incoming,
    weight_sem, send_sem, recv_sem, swap_send, swap_recv,
):
    position, index = order
    n = incoming.shape[0]
    half, part = incoming.shape[3], incoming.shape[4]
    width = 2 * part
    me = lax.axis_index("tensor")
    worker = lax.axis_index("worker")
    workers = everyone.shape[0]
    place = position(me)
    forward = index(lax.rem(place + 1, n))
    back = index(lax.rem(place + n - 1, n))
    targets = (forward, back)
    streams = [(d, c) for c in range(2) for d in range(2)]

    barrier = pltpu.get_barrier_semaphore()
    for target in targets:
        pl.semaphore_signal(barrier, inc=1, device_id={"tensor": target}, device_id_type=MESH)
    for k in range(1, workers):
        pl.semaphore_signal(
            barrier,
            inc=1,
            device_id={"worker": lax.rem(worker + k, workers)},
            device_id_type=MESH,
        )

    def weight_copy(block):
        cols = pl.ds(pl.multiple_of(block * width, width), width)
        return pltpu.make_async_copy(
            weight.at[:, cols], weight_all.at[block], weight_sem.at[block]
        )

    def start_weights(k, carry):
        weight_copy(index(lax.rem(place + n - 1 - k, n))).start()

        @pl.when(k < n // 2 - 1)
        def _():
            weight_copy(index(lax.rem(place + 1 + k, n))).start()

        return carry

    lax.fori_loop(0, n // 2, start_weights, 0)
    weight_copy(me).start()
    for d, c in streams:
        incoming[0, d, c] = jnp.zeros((half, part), jnp.bfloat16)
    pl.semaphore_wait(barrier, 1 + workers)

    def hop(step, d, c):
        return pltpu.make_async_remote_copy(
            src_ref=outgoing.at[step, d, c],
            dst_ref=incoming.at[step + 1, d, c],
            send_sem=send_sem.at[step, d, c],
            recv_sem=recv_sem.at[step + 1, d, c],
            device_id={"tensor": targets[d]},
            device_id_type=MESH,
        )

    def arrival(step, d, c):
        return pltpu.make_async_remote_copy(
            src_ref=outgoing.at[step, d, c],
            dst_ref=incoming.at[step, d, c],
            send_sem=send_sem.at[step, d, c],
            recv_sem=recv_sem.at[step, d, c],
            device_id={"tensor": targets[d]},
            device_id_type=MESH,
        )

    def step_body(step, carry):
        blocks = (
            index(lax.rem(place + 2 * n - 1 - step, n)),
            index(lax.rem(place + 1 + step, n)),
        )

        @pl.when(step < n // 2)
        def _():
            weight_copy(blocks[0]).wait()

        @pl.when(step < n // 2 - 1)
        def _():
            weight_copy(blocks[1]).wait()

        @pl.when(step == n // 2)
        def _():
            weight_copy(me).wait()

        for d, c in streams:
            product = jnp.dot(
                mixture[d * half : (d + 1) * half, :],
                weight_all[blocks[d], :, c * part : (c + 1) * part],
                preferred_element_type=jnp.float32,
            )

            @pl.when(step > 0)
            def _():
                arrival(step, d, c).wait_recv()

            summed = product + incoming[step, d, c].astype(jnp.float32)
            outgoing[step, d, c] = summed.astype(jnp.bfloat16)

            @pl.when(step < n - 1)
            def _():
                hop(step, d, c).start()

        return carry

    lax.fori_loop(0, n, step_body, 0)

    swaps = []
    for d in range(2):
        lines = slice(d * half, (d + 1) * half)
        for c in range(2):
            everyone[worker, lines, c * part : (c + 1) * part] = outgoing[n - 1, d, c]
        for k in range(1, workers):
            swap = pltpu.make_async_remote_copy(
                src_ref=everyone.at[worker, pl.ds(d * half, half)],
                dst_ref=everyone.at[worker, pl.ds(d * half, half)],
                send_sem=swap_send.at[k, d],
                recv_sem=swap_recv.at[k, d],
                device_id={"worker": lax.rem(worker + k, workers)},
                device_id_type=MESH,
            )
            swap.start()
            swaps.append(swap)

    def finish(step, carry):
        for d, c in streams:
            hop(step, d, c).wait_send()
        return carry

    lax.fori_loop(0, n - 1, finish, 0)
    for swap in swaps:
        swap.wait()


def project_out(order, n, workers, mixture, weight):
    rows, depth = mixture.shape
    width = weight.shape[1] // n
    half, part = rows // 2, width // 2
    vmem = pl.BlockSpec(memory_space=pltpu.VMEM)
    return pl.pallas_call(
        functools.partial(output_kernel, order),
        out_shape=jax.ShapeDtypeStruct((workers, rows, width), jnp.bfloat16),
        in_specs=[vmem, pl.BlockSpec(memory_space=pl.ANY)],
        out_specs=vmem,
        scratch_shapes=[
            pltpu.VMEM((n, depth, width), jnp.bfloat16),
            pltpu.VMEM((n, 2, 2, half, part), jnp.bfloat16),
            pltpu.VMEM((n, 2, 2, half, part), jnp.bfloat16),
            pltpu.SemaphoreType.DMA((n,)),
            pltpu.SemaphoreType.DMA((n, 2, 2)),
            pltpu.SemaphoreType.DMA((n, 2, 2)),
            pltpu.SemaphoreType.DMA((workers, 2)),
            pltpu.SemaphoreType.DMA((workers, 2)),
        ],
        compiler_params=pltpu.CompilerParams(
            collective_id=1, has_side_effects=True, vmem_limit_bytes=48 * 2**20
        ),
        name="project_out",
    )(mixture, weight)


def from_partner(block, axis, bit):
    count = lax.axis_size(axis)
    route = []
    for low in range(count):
        high = low | 1 << bit
        if high != low and high < count:
            route += [(low, high), (high, low)]
    return lax.ppermute(block, axis, route)


def whole_head(block, bits):
    me = lax.axis_index("tensor")
    for bit in range(bits):
        other = from_partner(block, "tensor", bit)
        upper = me // (1 << bit) % 2 == 1
        block = jnp.where(
            upper,
            jnp.concatenate([other, block], axis=1),
            jnp.concatenate([block, other], axis=1),
        )
    return block


def local(
    order,
    tokens,
    norm_gain,
    query_weight,
    key_weight,
    value_weight,
    output_weight,
    cached_blocks,
    cache_length,
    block_table,
    destination,
):
    n = lax.axis_size("tensor")
    workers = lax.axis_size("worker")
    worker_index = lax.axis_index("worker")
    seq_total = destination.shape[0]
    seqs, stored = cached_blocks.shape[0], cached_blocks.shape[1]
    lengths = lax.dynamic_slice_in_dim(cache_length, worker_index * seqs, seqs, 0)
    tables = lax.dynamic_slice_in_dim(block_table, worker_index * seqs, seqs, 0)

    halfway = HD // 2
    inverse = 500000.0 ** (-(jnp.arange(halfway, dtype=jnp.float32) * 2.0 / HD))
    positions = (lengths[:, None] + jnp.arange(NEW, dtype=jnp.int32)[None, :]).astype(jnp.float32)
    angles = positions.reshape(seqs * NEW, 1) * jnp.concatenate([inverse, inverse])[None, :]
    sign = jnp.where(jnp.arange(HD) < halfway, -1.0, 1.0)[None, :]
    cosine = jnp.cos(angles)
    sine = jnp.sin(angles) * sign

    logical = tables[:, :, None] * BLK + jnp.arange(BLK, dtype=jnp.int32)[None, None, :]
    seen = (logical < lengths[:, None, None]).astype(jnp.float32).reshape(seqs, 1, -1)

    kvt = cached_blocks.reshape(seqs, stored, 2, KVH, HD).transpose(3, 0, 2, 1, 4)
    query, key_raw, value, old = project(
        order, n, tokens, norm_gain[None, :], cosine, sine,
        query_weight, key_weight, value_weight, kvt,
    )
    bits = (n // KVH).bit_length() - 1
    key_raw, value = whole_head(key_raw, bits), whole_head(value, bits)
    mixture = attention(query, old, key_raw, value, cosine, sine, seen)
    everyone = project_out(order, n, workers, mixture, output_weight)
    everyone = everyone.reshape(seq_total, NEW, -1)

    belongs = destination == worker_index
    ranking = jnp.cumsum(belongs.astype(jnp.int32)) - 1
    result = jnp.zeros((CAP,) + everyone.shape[1:], everyone.dtype)
    slots = jnp.arange(CAP, dtype=jnp.int32)
    for seq in range(seq_total):
        chosen = belongs[seq] & (ranking[seq] == slots)
        result = jnp.where(chosen[:, None, None], everyone[seq][None], result)
    return result[None]


def solution(mesh):
    placed = (
        P(("groups", "worker"), "tensor"),
        P(),
        P(None, "tensor"),
        P(None, "tensor"),
        P(None, "tensor"),
        P("tensor", None),
        P(("groups", "worker"), "tensor", None, None),
        P("groups"),
        P("groups", None),
        P("groups"),
    )
    return jax.shard_map(
        functools.partial(local, ring_order(mesh)),
        mesh=mesh,
        in_specs=placed,
        out_specs=P(("groups", "worker"), None, None, "tensor"),
        check_vma=False,
    )
```

```python
import functools
import math

import jax
import jax.numpy as jnp
import numpy as np
from jax import lax
from jax.experimental import pallas as pl
from jax.experimental.pallas import tpu as pltpu
from jax.sharding import PartitionSpec as P

HD = 128
NEW = 128
BLK = 16
CAP = 3
KVH = 8

MESH = pl.DeviceIdType.MESH
epsilon = 1e-05


def snake_order(count):
    def position(index):
        column, row = lax.rem(index, 2), lax.div(index, 2)
        return row + column * (count - 1 - 2 * row)

    def index(place):
        second = lax.div(place, count // 2)
        return second * (2 * (count - 1 - place) + 1) + (1 - second) * (2 * place)

    return position, index


def layout(mesh):
    devices = mesh.devices[0, 0]
    count = devices.shape[0]
    places = [getattr(device, "coords", None) for device in devices]
    if count > 2 and count % 2 == 0 and all(place is not None for place in places):
        ring = list(range(0, count, 2)) + list(range(count - 1, 0, -2))
        steps = [
            sum(abs(a - b) for a, b in zip(places[ring[k]], places[ring[(k + 1) % count]]))
            for k in range(count)
        ]
        if max(steps) == 1:
            return snake_order(count), (count // 2, 2, False)
    return ((lambda index: index), (lambda place: place)), (count, 1, True)


def project_kernel(
    grid, seqs, tok, gain_hbm, inverse, lengths, wq, wk, wv, cached,
    q_out, k_out, v_out, cosine, sine, ctx,
    xg, gain, raw, kvt, wq_all, wk_all, wv_all, qacc, kacc, vacc, squares,
    weight_sem, send_sem, recv_sem, old_send, old_recv, own_sem, load_sem,
):
    lines, columns, wraps = grid
    n, parts, rows, part = xg.shape
    width = parts * part
    share = n // kvt.shape[0]
    me = lax.axis_index("tensor")
    worker = lax.axis_index("worker")
    line, column = lax.div(me, columns), lax.rem(me, columns)
    other = columns - 1 - column
    reach = lines // 2 + 1 if wraps else lines

    def source(k, side, where):
        moved = line + lines + (2 * side - 1) * k
        return lax.rem(moved, lines) * columns + where

    def comes(k, side):
        if wraps:
            return k + side <= lines // 2
        from_below = (1 - side) * (line - k)
        from_above = side * (lines - 1 - line - k)
        return from_below + from_above >= 0

    def goes_on(k, side):
        if wraps:
            return k + side < lines // 2
        return (1 - side) * (lines - 1 - line) + side * line > 0

    def neighbour(side):
        return lax.rem(line + lines + 1 - 2 * side, lines) * columns + column

    across = line * columns + other

    def weight_copies(block):
        span = pl.ds(pl.multiple_of(block * width, width), width)
        return [
            pltpu.make_async_copy(src.at[span, :], dst.at[block], weight_sem.at[block, k])
            for k, (src, dst) in enumerate(((wq, wq_all), (wk, wk_all), (wv, wv_all)))
        ]

    def start_weights(block):
        for copy in weight_copies(block):
            copy.start()

    barrier = pltpu.get_barrier_semaphore()

    def greet(k, carry):
        pl.semaphore_signal(
            barrier, inc=1, device_id={"tensor": lax.rem(me + k, n)}, device_id_type=MESH
        )
        return carry

    lax.fori_loop(1, n, greet, 0)

    def own_part(c):
        span = pl.ds(pl.multiple_of(c * part, part), part)
        return tok.at[:, span]

    own_parts = [
        pltpu.make_async_copy(own_part(c), xg.at[me, c], load_sem.at[c]) for c in range(parts)
    ]
    for copy in own_parts:
        copy.start()
    load_gain = pltpu.make_async_copy(gain_hbm, gain, load_sem.at[parts])
    load_gain.start()
    load_cached = pltpu.make_async_copy(cached, raw, load_sem.at[parts + 1])
    load_cached.start()
    start_weights(me)

    def spread(k, carry):
        for side in range(2):

            @pl.when(comes(k, side))
            def _():
                start_weights(source(k, side, column))

        return carry

    lax.fori_loop(1, reach, spread, 0)
    pl.semaphore_wait(barrier, n - 1)

    def remote(src, block, c, way, target):
        return pltpu.make_async_remote_copy(
            src_ref=src,
            dst_ref=xg.at[block, c],
            send_sem=send_sem.at[way, block, c],
            recv_sem=recv_sem.at[block, c],
            device_id={"tensor": target},
            device_id_type=MESH,
        )

    def own_hops(c):
        hops = [(goes_on(0, side), remote(own_part(c), me, c, side, neighbour(side))) for side in range(2)]
        if columns > 1:
            hops.append((True, remote(own_part(c), me, c, 2, across)))
        return hops

    for c in range(parts):
        for needed, copy in own_hops(c):
            pl.when(needed)(copy.start)

    def onward(k, side, block, c):
        hops = [(goes_on(k, side), remote(xg.at[block, c], block, c, side, neighbour(side)))]
        if columns > 1:
            hops.append((True, remote(xg.at[block, c], block, c, 2, across)))
        return hops

    def spread_across(k, carry):
        for side in range(2):

            @pl.when(comes(k, side) & (k + 1 > side))
            def _():
                start_weights(source(k, side, other))

        return carry

    if columns > 1:
        start_weights(across)
        lax.fori_loop(1, reach, spread_across, 0)

    load_cached.wait()
    for seq in range(raw.shape[0]):
        for kind in range(2):
            for head in range(kvt.shape[0]):
                kvt[head, seq, kind] = raw[seq, :, kind, head * HD : (head + 1) * HD]

    def stored(k):
        target = lax.rem(me + k, n)
        return pltpu.make_async_remote_copy(
            src_ref=kvt.at[lax.div(target, share)],
            dst_ref=ctx.at[me],
            send_sem=old_send.at[k],
            recv_sem=old_recv.at[k],
            device_id={"tensor": target},
            device_id_type=MESH,
        )

    def stored_arrival(k):
        origin = lax.rem(me + n - k, n)
        return pltpu.make_async_remote_copy(
            src_ref=kvt.at[0],
            dst_ref=ctx.at[origin],
            send_sem=old_send.at[k],
            recv_sem=old_recv.at[k],
            device_id={"tensor": origin},
            device_id_type=MESH,
        )

    own = pltpu.make_async_copy(kvt.at[lax.div(me, share)], ctx.at[me], own_sem)
    own.start()
    each = -(-(n - 1) // reach)

    def send_stored(k):
        for extra in range(each):
            number = 1 + k * each + extra

            @pl.when(number < n)
            def _():
                stored(number).start()

    qacc[...] = jnp.zeros_like(qacc)
    kacc[...] = jnp.zeros_like(kacc)
    vacc[...] = jnp.zeros_like(vacc)
    squares[...] = jnp.zeros_like(squares)

    def multiply(block, c):
        @pl.when(c == 0)
        def _():
            for copy in weight_copies(block):
                copy.wait()

        values = xg[block, c].astype(jnp.float32)
        squares[...] += jnp.sum(values * values, axis=1, keepdims=True)
        offset = pl.multiple_of(block * width + c * part, part)
        scaled = (values * gain[:, pl.ds(offset, part)]).astype(jnp.bfloat16)
        span = pl.ds(pl.multiple_of(c * part, part), part)
        for total, weight in ((qacc, wq_all), (kacc, wk_all), (vacc, wv_all)):
            total[...] += jnp.dot(
                scaled, weight[block, span, :], preferred_element_type=jnp.float32
            )

    load_gain.wait()
    for copy in own_parts:
        copy.wait()
    send_stored(0)

    def own_body(c, carry):
        multiply(me, c)
        return carry

    lax.fori_loop(0, parts, own_body, 0)

    for seq in range(seqs):
        span = slice(seq * NEW, (seq + 1) * NEW)
        start = lengths[worker * seqs + seq]
        position = start + lax.broadcasted_iota(jnp.int32, (NEW, HD), 0)
        angle = position.astype(jnp.float32) * inverse[...]
        lane = lax.broadcasted_iota(jnp.int32, (NEW, HD), 1)
        cosine[span, :] = jnp.cos(angle)
        turn = jnp.sin(angle)
        sine[span, :] = jnp.where(lane < HD // 2, -turn, turn)

    def arrive(block, c):
        remote(xg.at[block, c], block, c, 0, across).wait_recv()

    def along(k, carry):
        send_stored(k)

        def piece(number, carry):
            c, side = lax.div(number, 2), lax.rem(number, 2)
            block = source(k, side, column)

            @pl.when(comes(k, side))
            def _():
                arrive(block, c)
                for needed, copy in onward(k, side, block, c):
                    pl.when(needed)(copy.start)
                multiply(block, c)

            return carry

        return lax.fori_loop(0, 2 * parts, piece, carry)

    lax.fori_loop(1, reach, along, 0)

    def beyond(k, carry):
        def piece(number, carry):
            c, side = lax.div(number, 2), lax.rem(number, 2)
            block = source(k, side, other)

            @pl.when(comes(k, side) & (k + 1 > side))
            def _():
                arrive(block, c)
                multiply(block, c)

            return carry

        return lax.fori_loop(0, 2 * parts, piece, carry)

    if columns > 1:
        lax.fori_loop(0, reach, beyond, 0)

    factor = lax.rsqrt(squares[...] / (n * width) + epsilon)
    k_out[...] = (kacc[...] * factor).astype(jnp.bfloat16)
    v_out[...] = (vacc[...] * factor).astype(jnp.bfloat16)
    for head in range(q_out.shape[1] // HD):
        cols = slice(head * HD, (head + 1) * HD)
        query = qacc[:, cols] * factor
        turned = pltpu.roll(query, HD // 2, 1)
        q_out[:, cols] = (query * cosine[...] + turned * sine[...]).astype(jnp.bfloat16)

    for c in range(parts):
        for needed, copy in own_hops(c):
            pl.when(needed)(copy.wait_send)

    def sent(k, carry):
        def piece(number, carry):
            c, side = lax.div(number, 2), lax.rem(number, 2)
            block = source(k, side, column)

            @pl.when(comes(k, side))
            def _():
                for needed, copy in onward(k, side, block, c):
                    pl.when(needed)(copy.wait_send)

            return carry

        return lax.fori_loop(0, 2 * parts, piece, carry)

    lax.fori_loop(1, reach, sent, 0)

    def finish(k, carry):
        stored(k).wait_send()
        stored_arrival(k).wait_recv()
        return carry

    lax.fori_loop(1, n, finish, 0)
    own.wait()


def project(grid, n, tokens, gain, inverse, lengths, wq, wk, wv, cached):
    rows, width = tokens.shape
    part = max(HD, width // 4)
    parts = width // part
    cols, narrow = wq.shape[1], wk.shape[1]
    seqs, stored = cached.shape[0], cached.shape[1]
    vmem = pl.BlockSpec(memory_space=pltpu.VMEM)
    smem = pl.BlockSpec(memory_space=pltpu.SMEM)
    anywhere = pl.BlockSpec(memory_space=pl.ANY)
    kvt = (KVH, seqs, 2, stored, HD)
    ways = 2 + (grid[1] > 1)
    return pl.pallas_call(
        functools.partial(project_kernel, grid, seqs),
        out_shape=(
            jax.ShapeDtypeStruct((rows, cols), jnp.bfloat16),
            jax.ShapeDtypeStruct((rows, narrow), jnp.bfloat16),
            jax.ShapeDtypeStruct((rows, narrow), jnp.bfloat16),
            jax.ShapeDtypeStruct((rows, HD), jnp.float32),
            jax.ShapeDtypeStruct((rows, HD), jnp.float32),
            jax.ShapeDtypeStruct((n,) + kvt[1:], jnp.bfloat16),
        ),
        in_specs=[anywhere, anywhere, vmem, smem] + [anywhere] * 4,
        out_specs=(vmem,) * 5 + (anywhere,),
        scratch_shapes=[
            pltpu.VMEM((n, parts, rows, part), jnp.bfloat16),
            pltpu.VMEM(gain.shape, jnp.float32),
            pltpu.VMEM(cached.shape, jnp.bfloat16),
            pltpu.VMEM(kvt, jnp.bfloat16),
            pltpu.VMEM((n, width, cols), jnp.bfloat16),
            pltpu.VMEM((n, width, narrow), jnp.bfloat16),
            pltpu.VMEM((n, width, narrow), jnp.bfloat16),
            pltpu.VMEM((rows, cols), jnp.float32),
            pltpu.VMEM((rows, narrow), jnp.float32),
            pltpu.VMEM((rows, narrow), jnp.float32),
            pltpu.VMEM((rows, 1), jnp.float32),
            pltpu.SemaphoreType.DMA((n, 3)),
            pltpu.SemaphoreType.DMA((ways, n, parts)),
            pltpu.SemaphoreType.DMA((n, parts)),
            pltpu.SemaphoreType.DMA((n,)),
            pltpu.SemaphoreType.DMA((n,)),
            pltpu.SemaphoreType.DMA,
            pltpu.SemaphoreType.DMA((parts + 2,)),
        ],
        compiler_params=pltpu.CompilerParams(
            collective_id=0, has_side_effects=True, vmem_limit_bytes=60 * 2**20
        ),
        name="gather_project",
    )(tokens, gain, inverse, lengths, wq, wk, wv, cached)


def attend_kernel(query, old, key_raw, value, cosine, sine, bias, mixture, key_turned):
    @pl.when(pl.program_id(1) == 0)
    def _():
        raw = key_raw[...].astype(jnp.float32)
        turned = pltpu.roll(raw, HD // 2, 1)
        key_turned[...] = (raw * cosine[...] + turned * sine[...]).astype(jnp.bfloat16)

    heads = query.shape[1] // HD
    count = old.shape[0] * old.shape[3]
    old_key = old[:, 0, 0].reshape(count, HD)
    old_value = old[:, 0, 1].reshape(count, HD)
    scale = math.log2(math.e) / math.sqrt(HD)
    contract = (((1,), (1,)), ((), ()))
    seen = bias[0] > 0
    row = lax.broadcasted_iota(jnp.int32, (NEW, NEW), 0)
    col = lax.broadcasted_iota(jnp.int32, (NEW, NEW), 1)
    for head in range(heads):
        cols = slice(head * HD, (head + 1) * HD)
        one = query[:, cols]
        old_scores = lax.dot_general(one, old_key, contract, preferred_element_type=jnp.float32)
        new_scores = lax.dot_general(
            one, key_turned[...], contract, preferred_element_type=jnp.float32
        )
        old_scores = jnp.where(seen, old_scores * scale, -1e30)
        new_scores = jnp.where(row >= col, new_scores * scale, -1e30)
        largest = jnp.maximum(
            jnp.max(old_scores, axis=1, keepdims=True),
            jnp.max(new_scores, axis=1, keepdims=True),
        )
        old_expo = jnp.exp2(old_scores - largest)
        new_expo = jnp.exp2(new_scores - largest)
        inverse = 1.0 / (
            jnp.sum(old_expo, axis=1, keepdims=True) + jnp.sum(new_expo, axis=1, keepdims=True)
        )
        old_probs = (old_expo * inverse).astype(jnp.bfloat16)
        new_probs = (new_expo * inverse).astype(jnp.bfloat16)
        mixed = jnp.dot(old_probs, old_value, preferred_element_type=jnp.float32)
        mixed += jnp.dot(new_probs, value[...], preferred_element_type=jnp.float32)
        mixture[:, cols] = mixed.astype(jnp.bfloat16)


def attention(query, old, key_raw, value, cosine, sine, bias):
    seqs = old.shape[1]
    heads = query.shape[1] // HD
    together = math.gcd(heads, 4)
    per_seq = pl.BlockSpec((NEW, HD), lambda s, h: (s, 0))
    per_head = pl.BlockSpec((NEW, HD * together), lambda s, h: (s, h))
    return pl.pallas_call(
        attend_kernel,
        out_shape=jax.ShapeDtypeStruct(query.shape, jnp.bfloat16),
        grid=(seqs, heads // together),
        in_specs=[
            per_head,
            pl.BlockSpec((old.shape[0], 1) + old.shape[2:], lambda s, h: (0, s, 0, 0, 0)),
            per_seq,
            per_seq,
            per_seq,
            per_seq,
            pl.BlockSpec((1, 1, bias.shape[2]), lambda s, h: (s, 0, 0)),
        ],
        out_specs=per_head,
        scratch_shapes=[pltpu.VMEM((NEW, HD), jnp.bfloat16)],
        compiler_params=pltpu.CompilerParams(vmem_limit_bytes=48 * 2**20),
        name="attention",
    )(query, old, key_raw, value, cosine, sine, bias)


def output_kernel(
    order, mixture, weight, destination, result,
    everyone, weight_all, outgoing, incoming,
    weight_sem, send_sem, recv_sem, swap_send, swap_recv,
):
    position, index = order
    n = incoming.shape[0]
    half, part = incoming.shape[3], incoming.shape[4]
    width = 2 * part
    me = lax.axis_index("tensor")
    worker = lax.axis_index("worker")
    workers = everyone.shape[0]
    place = position(me)
    forward = index(lax.rem(place + 1, n))
    back = index(lax.rem(place + n - 1, n))
    targets = (forward, back)
    streams = [(d, c) for c in range(2) for d in range(2)]

    barrier = pltpu.get_barrier_semaphore()
    for target in targets:
        pl.semaphore_signal(barrier, inc=1, device_id={"tensor": target}, device_id_type=MESH)
    for k in range(1, workers):
        pl.semaphore_signal(
            barrier,
            inc=1,
            device_id={"worker": lax.rem(worker + k, workers)},
            device_id_type=MESH,
        )

    def weight_copy(block):
        cols = pl.ds(pl.multiple_of(block * width, width), width)
        return pltpu.make_async_copy(
            weight.at[:, cols], weight_all.at[block], weight_sem.at[block]
        )

    def start_weights(k, carry):
        weight_copy(index(lax.rem(place + n - 1 - k, n))).start()

        @pl.when(k < n // 2 - 1)
        def _():
            weight_copy(index(lax.rem(place + 1 + k, n))).start()

        return carry

    lax.fori_loop(0, n // 2, start_weights, 0)
    weight_copy(me).start()
    for d, c in streams:
        incoming[0, d, c] = jnp.zeros((half, part), jnp.bfloat16)
    pl.semaphore_wait(barrier, 1 + workers)

    def hop(step, d, c):
        return pltpu.make_async_remote_copy(
            src_ref=outgoing.at[step, d, c],
            dst_ref=incoming.at[step + 1, d, c],
            send_sem=send_sem.at[step, d, c],
            recv_sem=recv_sem.at[step + 1, d, c],
            device_id={"tensor": targets[d]},
            device_id_type=MESH,
        )

    def arrival(step, d, c):
        return pltpu.make_async_remote_copy(
            src_ref=outgoing.at[step, d, c],
            dst_ref=incoming.at[step, d, c],
            send_sem=send_sem.at[step, d, c],
            recv_sem=recv_sem.at[step, d, c],
            device_id={"tensor": targets[d]},
            device_id_type=MESH,
        )

    def step_body(step, carry):
        blocks = (
            index(lax.rem(place + 2 * n - 1 - step, n)),
            index(lax.rem(place + 1 + step, n)),
        )

        @pl.when(step < n // 2)
        def _():
            weight_copy(blocks[0]).wait()

        @pl.when(step < n // 2 - 1)
        def _():
            weight_copy(blocks[1]).wait()

        @pl.when(step == n // 2)
        def _():
            weight_copy(me).wait()

        for d, c in streams:
            product = jnp.dot(
                mixture[d * half : (d + 1) * half, :],
                weight_all[blocks[d], :, c * part : (c + 1) * part],
                preferred_element_type=jnp.float32,
            )

            @pl.when(step > 0)
            def _():
                arrival(step, d, c).wait_recv()

            summed = product + incoming[step, d, c].astype(jnp.float32)
            outgoing[step, d, c] = summed.astype(jnp.bfloat16)

            @pl.when(step < n - 1)
            def _():
                hop(step, d, c).start()

        return carry

    lax.fori_loop(0, n, step_body, 0)

    swaps = []
    for d in range(2):
        lines = slice(d * half, (d + 1) * half)
        for c in range(2):
            everyone[worker, lines, c * part : (c + 1) * part] = outgoing[n - 1, d, c]
        for k in range(1, workers):
            swap = pltpu.make_async_remote_copy(
                src_ref=everyone.at[worker, pl.ds(d * half, half)],
                dst_ref=everyone.at[worker, pl.ds(d * half, half)],
                send_sem=swap_send.at[k, d],
                recv_sem=swap_recv.at[k, d],
                device_id={"worker": lax.rem(worker + k, workers)},
                device_id_type=MESH,
            )
            swap.start()
            swaps.append(swap)

    def finish(step, carry):
        for d, c in streams:
            hop(step, d, c).wait_send()
        return carry

    lax.fori_loop(0, n - 1, finish, 0)
    for swap in swaps:
        swap.wait()

    seqs = destination.shape[0]
    local_seqs = seqs // workers
    bound = [jnp.where(destination[seq] == worker, 1, 0) for seq in range(seqs)]
    rank, ranks = 0, []
    for seq in range(seqs):
        ranks.append(rank)
        rank = rank + bound[seq]
    for slot in range(result.shape[0]):
        chosen = [jnp.where(ranks[seq] == slot, bound[seq], 0) for seq in range(seqs)]
        picked = jnp.zeros(result.shape[1:], result.dtype)
        for seq in range(seqs):
            first = seq % local_seqs * NEW
            rows = everyone[seq // local_seqs, first : first + NEW, :]
            flag = jnp.full(result.shape[1:], chosen[seq], jnp.int32)
            picked = jnp.where(flag > 0, rows, picked)
        result[slot] = picked


def project_out(order, n, workers, mixture, weight, destination):
    rows, depth = mixture.shape
    width = weight.shape[1] // n
    half, part = rows // 2, width // 2
    vmem = pl.BlockSpec(memory_space=pltpu.VMEM)
    return pl.pallas_call(
        functools.partial(output_kernel, order),
        out_shape=jax.ShapeDtypeStruct((CAP, NEW, width), jnp.bfloat16),
        in_specs=[
            vmem,
            pl.BlockSpec(memory_space=pl.ANY),
            pl.BlockSpec(memory_space=pltpu.SMEM),
        ],
        out_specs=vmem,
        scratch_shapes=[
            pltpu.VMEM((workers, rows, width), jnp.bfloat16),
            pltpu.VMEM((n, depth, width), jnp.bfloat16),
            pltpu.VMEM((n, 2, 2, half, part), jnp.bfloat16),
            pltpu.VMEM((n, 2, 2, half, part), jnp.bfloat16),
            pltpu.SemaphoreType.DMA((n,)),
            pltpu.SemaphoreType.DMA((n, 2, 2)),
            pltpu.SemaphoreType.DMA((n, 2, 2)),
            pltpu.SemaphoreType.DMA((workers, 2)),
            pltpu.SemaphoreType.DMA((workers, 2)),
        ],
        compiler_params=pltpu.CompilerParams(
            collective_id=1, has_side_effects=True, vmem_limit_bytes=48 * 2**20
        ),
        name="project_out",
    )(mixture, weight, destination)


def from_partner(block, axis, bit):
    count = lax.axis_size(axis)
    route = []
    for low in range(count):
        high = low | 1 << bit
        if high != low and high < count:
            route += [(low, high), (high, low)]
    return lax.ppermute(block, axis, route)


def whole_head(block, bits):
    me = lax.axis_index("tensor")
    for bit in range(bits):
        other = from_partner(block, "tensor", bit)
        upper = me // (1 << bit) % 2 == 1
        block = jnp.where(
            upper,
            jnp.concatenate([other, block], axis=1),
            jnp.concatenate([block, other], axis=1),
        )
    return block


def local(
    ring,
    grid,
    tokens,
    norm_gain,
    query_weight,
    key_weight,
    value_weight,
    output_weight,
    cached_blocks,
    cache_length,
    block_table,
    destination,
):
    n = lax.axis_size("tensor")
    workers = lax.axis_size("worker")
    seqs = cached_blocks.shape[0]
    first = lax.axis_index("worker") * seqs
    lengths = lax.dynamic_slice_in_dim(cache_length, first, seqs, 0)
    tables = lax.dynamic_slice_in_dim(block_table, first, seqs, 0)
    logical = tables[:, :, None] * BLK + jnp.arange(BLK, dtype=jnp.int32)[None, None, :]
    seen = (logical < lengths[:, None, None]).astype(jnp.float32).reshape(seqs, 1, -1)

    half = 500000.0 ** (-(np.arange(HD // 2) * 2.0 / HD))
    inverse = jnp.asarray(np.concatenate([half, half])[None, :], jnp.float32)
    query, key_raw, value, cosine, sine, old = project(
        grid, n, tokens, norm_gain[None, :], inverse, cache_length,
        query_weight, key_weight, value_weight, cached_blocks,
    )
    bits = (n // KVH).bit_length() - 1
    key_raw, value = whole_head(key_raw, bits), whole_head(value, bits)
    mixture = attention(query, old, key_raw, value, cosine, sine, seen)
    return project_out(ring, n, workers, mixture, output_weight, destination)[None]


def solution(mesh):
    placed = (
        P(("groups", "worker"), "tensor"),
        P(),
        P(None, "tensor"),
        P(None, "tensor"),
        P(None, "tensor"),
        P("tensor", None),
        P(("groups", "worker"), "tensor", None, None),
        P("groups"),
        P("groups", None),
        P("groups"),
    )
    return jax.shard_map(
        functools.partial(local, *layout(mesh)),
        mesh=mesh,
        in_specs=placed,
        out_specs=P(("groups", "worker"), None, None, "tensor"),
        check_vma=False,
    )
```

```python
import functools
import math

import jax
import jax.numpy as jnp
import numpy as np
from jax import lax
from jax.experimental import pallas as pl
from jax.experimental.pallas import tpu as pltpu
from jax.sharding import PartitionSpec as P

HD = 128
NEW = 128
BLK = 16
CAP = 3
KVH = 8

MESH = pl.DeviceIdType.MESH
epsilon = 1e-05


def snake_order(count):
    def position(index):
        column, row = lax.rem(index, 2), lax.div(index, 2)
        return row + column * (count - 1 - 2 * row)

    def index(place):
        second = lax.div(place, count // 2)
        return second * (2 * (count - 1 - place) + 1) + (1 - second) * (2 * place)

    return position, index


def layout(mesh):
    devices = mesh.devices[0, 0]
    count = devices.shape[0]
    places = [getattr(device, "coords", None) for device in devices]
    if count > 2 and count % 2 == 0 and all(place is not None for place in places):
        ring = list(range(0, count, 2)) + list(range(count - 1, 0, -2))
        steps = [
            sum(abs(a - b) for a, b in zip(places[ring[k]], places[ring[(k + 1) % count]]))
            for k in range(count)
        ]
        if max(steps) == 1:
            return snake_order(count), (count // 2, 2, False)
    return ((lambda index: index), (lambda place: place)), (count, 1, True)


def project_kernel(
    grid, seqs, greet_workers, after_weights, tok, gain_hbm, inverse, lengths, wq, wk, wv, cached,
    q_out, k_out, v_out, cosine, sine, ctx,
    xg, gain, raw, kvt, wq_all, wk_all, wv_all, qacc, kacc, vacc, squares,
    weight_sem, send_sem, recv_sem, old_send, old_recv, own_sem, load_sem,
):
    lines, columns, wraps = grid
    n, parts, rows, part = xg.shape
    width = parts * part
    share = n // kvt.shape[0]
    me = lax.axis_index("tensor")
    worker = lax.axis_index("worker")
    line, column = lax.div(me, columns), lax.rem(me, columns)
    other = columns - 1 - column
    reach = lines // 2 + 1 if wraps else lines

    def source(k, side, where):
        moved = line + lines + (2 * side - 1) * k
        return lax.rem(moved, lines) * columns + where

    def comes(k, side):
        if wraps:
            return k + side <= lines // 2
        from_below = (1 - side) * (line - k)
        from_above = side * (lines - 1 - line - k)
        return from_below + from_above >= 0

    def goes_on(k, side):
        if wraps:
            return k + side < lines // 2
        return (1 - side) * (lines - 1 - line) + side * line > 0

    def neighbour(side):
        return lax.rem(line + lines + 1 - 2 * side, lines) * columns + column

    across = line * columns + other

    def weight_copies(block):
        span = pl.ds(pl.multiple_of(block * width, width), width)
        return [
            pltpu.make_async_copy(src.at[span, :], dst.at[block], weight_sem.at[block, k])
            for k, (src, dst) in enumerate(((wq, wq_all), (wk, wk_all), (wv, wv_all)))
        ]

    def start_weights(block):
        for copy in weight_copies(block):
            copy.start()

    barrier = pltpu.get_barrier_semaphore()

    def greet(k, carry):
        pl.semaphore_signal(
            barrier, inc=1, device_id={"tensor": lax.rem(me + k, n)}, device_id_type=MESH
        )
        return carry

    lax.fori_loop(1, n, greet, 0)
    workers = lax.axis_size("worker") if greet_workers else 1
    for k in range(1, workers):
        pl.semaphore_signal(
            barrier,
            inc=1,
            device_id={"worker": lax.rem(worker + k, workers)},
            device_id_type=MESH,
        )

    def own_part(c):
        span = pl.ds(pl.multiple_of(c * part, part), part)
        return tok.at[:, span]

    own_parts = [
        pltpu.make_async_copy(own_part(c), xg.at[me, c], load_sem.at[c]) for c in range(parts)
    ]
    for copy in own_parts:
        copy.start()
    load_gain = pltpu.make_async_copy(gain_hbm, gain, load_sem.at[parts])
    load_gain.start()
    load_cached = pltpu.make_async_copy(cached, raw, load_sem.at[parts + 1])
    load_cached.start()
    start_weights(me)

    def spread(k, carry):
        for side in range(2):

            @pl.when(comes(k, side))
            def _():
                start_weights(source(k, side, column))

        return carry

    lax.fori_loop(1, reach, spread, 0)
    pl.semaphore_wait(barrier, n - 2 + workers)

    def remote(src, block, c, way, target):
        return pltpu.make_async_remote_copy(
            src_ref=src,
            dst_ref=xg.at[block, c],
            send_sem=send_sem.at[way, block, c],
            recv_sem=recv_sem.at[block, c],
            device_id={"tensor": target},
            device_id_type=MESH,
        )

    def own_hops(c):
        hops = [(goes_on(0, side), remote(own_part(c), me, c, side, neighbour(side))) for side in range(2)]
        if columns > 1:
            hops.append((True, remote(own_part(c), me, c, 2, across)))
        return hops

    for c in range(parts):
        for needed, copy in own_hops(c):
            pl.when(needed)(copy.start)

    def onward(k, side, block, c):
        hops = [(goes_on(k, side), remote(xg.at[block, c], block, c, side, neighbour(side)))]
        if columns > 1:
            hops.append((True, remote(xg.at[block, c], block, c, 2, across)))
        return hops

    def spread_across(k, carry):
        for side in range(2):

            @pl.when(comes(k, side) & (k + 1 > side))
            def _():
                start_weights(source(k, side, other))

        return carry

    if columns > 1:
        start_weights(across)
        lax.fori_loop(1, reach, spread_across, 0)
    if after_weights is not None:
        after_weights()

    load_cached.wait()
    for seq in range(raw.shape[0]):
        for kind in range(2):
            for head in range(kvt.shape[0]):
                kvt[head, seq, kind] = raw[seq, :, kind, head * HD : (head + 1) * HD]

    def stored(k):
        target = lax.rem(me + k, n)
        return pltpu.make_async_remote_copy(
            src_ref=kvt.at[lax.div(target, share)],
            dst_ref=ctx.at[me],
            send_sem=old_send.at[k],
            recv_sem=old_recv.at[k],
            device_id={"tensor": target},
            device_id_type=MESH,
        )

    def stored_arrival(k):
        origin = lax.rem(me + n - k, n)
        return pltpu.make_async_remote_copy(
            src_ref=kvt.at[0],
            dst_ref=ctx.at[origin],
            send_sem=old_send.at[k],
            recv_sem=old_recv.at[k],
            device_id={"tensor": origin},
            device_id_type=MESH,
        )

    own = pltpu.make_async_copy(kvt.at[lax.div(me, share)], ctx.at[me], own_sem)
    own.start()

    def send_stored(k, carry):
        stored(k).start()
        return carry

    qacc[...] = jnp.zeros_like(qacc)
    kacc[...] = jnp.zeros_like(kacc)
    vacc[...] = jnp.zeros_like(vacc)
    squares[...] = jnp.zeros_like(squares)

    def multiply(block, c):
        @pl.when(c == 0)
        def _():
            for copy in weight_copies(block):
                copy.wait()

        values = xg[block, c].astype(jnp.float32)
        squares[...] += jnp.sum(values * values, axis=1, keepdims=True)
        offset = pl.multiple_of(block * width + c * part, part)
        scaled = (values * gain[:, pl.ds(offset, part)]).astype(jnp.bfloat16)
        span = pl.ds(pl.multiple_of(c * part, part), part)
        for total, weight in ((qacc, wq_all), (kacc, wk_all), (vacc, wv_all)):
            total[...] += jnp.dot(
                scaled, weight[block, span, :], preferred_element_type=jnp.float32
            )

    load_gain.wait()
    for copy in own_parts:
        copy.wait()

    def own_body(c, carry):
        multiply(me, c)
        return carry

    lax.fori_loop(0, parts, own_body, 0)

    for seq in range(seqs):
        span = slice(seq * NEW, (seq + 1) * NEW)
        start = lengths[worker * seqs + seq]
        position = start + lax.broadcasted_iota(jnp.int32, (NEW, HD), 0)
        angle = position.astype(jnp.float32) * inverse[...]
        lane = lax.broadcasted_iota(jnp.int32, (NEW, HD), 1)
        cosine[span, :] = jnp.cos(angle)
        turn = jnp.sin(angle)
        sine[span, :] = jnp.where(lane < HD // 2, -turn, turn)

    def arrive(block, c):
        remote(xg.at[block, c], block, c, 0, across).wait_recv()

    def along(k, carry):
        def piece(number, carry):
            c, side = lax.div(number, 2), lax.rem(number, 2)
            block = source(k, side, column)

            @pl.when(comes(k, side))
            def _():
                arrive(block, c)
                for needed, copy in onward(k, side, block, c):
                    pl.when(needed)(copy.start)
                multiply(block, c)

            return carry

        return lax.fori_loop(0, 2 * parts, piece, carry)

    lax.fori_loop(1, reach, along, 0)
    lax.fori_loop(1, n, send_stored, 0)

    def beyond(k, carry):
        def piece(number, carry):
            c, side = lax.div(number, 2), lax.rem(number, 2)
            block = source(k, side, other)

            @pl.when(comes(k, side) & (k + 1 > side))
            def _():
                arrive(block, c)
                multiply(block, c)

            return carry

        return lax.fori_loop(0, 2 * parts, piece, carry)

    if columns > 1:
        lax.fori_loop(0, reach, beyond, 0)

    factor = lax.rsqrt(squares[...] / (n * width) + epsilon)
    k_out[...] = (kacc[...] * factor).astype(jnp.bfloat16)
    v_out[...] = (vacc[...] * factor).astype(jnp.bfloat16)
    for head in range(q_out.shape[1] // HD):
        cols = slice(head * HD, (head + 1) * HD)
        query = qacc[:, cols] * factor
        turned = pltpu.roll(query, HD // 2, 1)
        q_out[:, cols] = (query * cosine[...] + turned * sine[...]).astype(jnp.bfloat16)

    for c in range(parts):
        for needed, copy in own_hops(c):
            pl.when(needed)(copy.wait_send)

    def sent(k, carry):
        def piece(number, carry):
            c, side = lax.div(number, 2), lax.rem(number, 2)
            block = source(k, side, column)

            @pl.when(comes(k, side))
            def _():
                for needed, copy in onward(k, side, block, c):
                    pl.when(needed)(copy.wait_send)

            return carry

        return lax.fori_loop(0, 2 * parts, piece, carry)

    lax.fori_loop(1, reach, sent, 0)

    def finish(k, carry):
        stored(k).wait_send()
        stored_arrival(k).wait_recv()
        return carry

    lax.fori_loop(1, n, finish, 0)
    own.wait()


def project_scratch(grid, n, tokens, gain, wq, wk, cached):
    rows, width = tokens.shape
    part = max(HD, width // 4)
    parts = width // part
    cols, narrow = wq.shape[1], wk.shape[1]
    ways = 2 + (grid[1] > 1)
    return [
        pltpu.VMEM((n, parts, rows, part), jnp.bfloat16),
        pltpu.VMEM(gain.shape, jnp.float32),
        pltpu.VMEM(cached.shape, jnp.bfloat16),
        pltpu.VMEM((KVH, cached.shape[0], 2, cached.shape[1], HD), jnp.bfloat16),
        pltpu.VMEM((n, width, cols), jnp.bfloat16),
        pltpu.VMEM((n, width, narrow), jnp.bfloat16),
        pltpu.VMEM((n, width, narrow), jnp.bfloat16),
        pltpu.VMEM((rows, cols), jnp.float32),
        pltpu.VMEM((rows, narrow), jnp.float32),
        pltpu.VMEM((rows, narrow), jnp.float32),
        pltpu.VMEM((rows, 1), jnp.float32),
        pltpu.SemaphoreType.DMA((n, 3)),
        pltpu.SemaphoreType.DMA((ways, n, parts)),
        pltpu.SemaphoreType.DMA((n, parts)),
        pltpu.SemaphoreType.DMA((n,)),
        pltpu.SemaphoreType.DMA((n,)),
        pltpu.SemaphoreType.DMA,
        pltpu.SemaphoreType.DMA((parts + 2,)),
    ]


def project(grid, n, tokens, gain, inverse, lengths, wq, wk, wv, cached):
    rows = tokens.shape[0]
    cols, narrow = wq.shape[1], wk.shape[1]
    seqs, stored = cached.shape[0], cached.shape[1]
    vmem = pl.BlockSpec(memory_space=pltpu.VMEM)
    smem = pl.BlockSpec(memory_space=pltpu.SMEM)
    anywhere = pl.BlockSpec(memory_space=pl.ANY)
    return pl.pallas_call(
        functools.partial(project_kernel, grid, seqs, False, None),
        out_shape=(
            jax.ShapeDtypeStruct((rows, cols), jnp.bfloat16),
            jax.ShapeDtypeStruct((rows, narrow), jnp.bfloat16),
            jax.ShapeDtypeStruct((rows, narrow), jnp.bfloat16),
            jax.ShapeDtypeStruct((rows, HD), jnp.float32),
            jax.ShapeDtypeStruct((rows, HD), jnp.float32),
            jax.ShapeDtypeStruct((n, seqs, 2, stored, HD), jnp.bfloat16),
        ),
        in_specs=[anywhere, anywhere, vmem, smem] + [anywhere] * 4,
        out_specs=(vmem,) * 5 + (anywhere,),
        scratch_shapes=project_scratch(grid, n, tokens, gain, wq, wk, cached),
        compiler_params=pltpu.CompilerParams(
            collective_id=0, has_side_effects=True, vmem_limit_bytes=60 * 2**20
        ),
        name="gather_project",
    )(tokens, gain, inverse, lengths, wq, wk, wv, cached)


def attend_heads(query, old_key, old_value, key, value, seen, mixture, heads, lines):
    scale = math.log2(math.e) / math.sqrt(HD)
    contract = (((1,), (1,)), ((), ()))
    row = lax.broadcasted_iota(jnp.int32, (NEW, NEW), 0)
    col = lax.broadcasted_iota(jnp.int32, (NEW, NEW), 1)
    for cols in heads:
        one = query[lines, cols]
        old_scores = lax.dot_general(one, old_key, contract, preferred_element_type=jnp.float32)
        new_scores = lax.dot_general(one, key, contract, preferred_element_type=jnp.float32)
        old_scores = jnp.where(seen, old_scores * scale, -1e30)
        new_scores = jnp.where(row >= col, new_scores * scale, -1e30)
        largest = jnp.maximum(
            jnp.max(old_scores, axis=1, keepdims=True),
            jnp.max(new_scores, axis=1, keepdims=True),
        )
        old_expo = jnp.exp2(old_scores - largest)
        new_expo = jnp.exp2(new_scores - largest)
        inverse = 1.0 / (
            jnp.sum(old_expo, axis=1, keepdims=True) + jnp.sum(new_expo, axis=1, keepdims=True)
        )
        old_probs = (old_expo * inverse).astype(jnp.bfloat16)
        new_probs = (new_expo * inverse).astype(jnp.bfloat16)
        mixed = jnp.dot(old_probs, old_value, preferred_element_type=jnp.float32)
        mixed += jnp.dot(new_probs, value, preferred_element_type=jnp.float32)
        mixture[lines, cols] = mixed.astype(jnp.bfloat16)


def attend_kernel(query, old, key_raw, value, cosine, sine, bias, mixture, key_turned):
    @pl.when(pl.program_id(1) == 0)
    def _():
        raw = key_raw[...].astype(jnp.float32)
        turned = pltpu.roll(raw, HD // 2, 1)
        key_turned[...] = (raw * cosine[...] + turned * sine[...]).astype(jnp.bfloat16)

    count = old.shape[0] * old.shape[3]
    attend_heads(
        query,
        old[:, 0, 0].reshape(count, HD),
        old[:, 0, 1].reshape(count, HD),
        key_turned[...],
        value[...],
        bias[0] > 0,
        mixture,
        [slice(head * HD, (head + 1) * HD) for head in range(query.shape[1] // HD)],
        slice(None),
    )


def attention(query, old, key_raw, value, cosine, sine, bias):
    seqs = old.shape[1]
    heads = query.shape[1] // HD
    together = math.gcd(heads, 4)
    per_seq = pl.BlockSpec((NEW, HD), lambda s, h: (s, 0))
    per_head = pl.BlockSpec((NEW, HD * together), lambda s, h: (s, h))
    return pl.pallas_call(
        attend_kernel,
        out_shape=jax.ShapeDtypeStruct(query.shape, jnp.bfloat16),
        grid=(seqs, heads // together),
        in_specs=[
            per_head,
            pl.BlockSpec((old.shape[0], 1) + old.shape[2:], lambda s, h: (0, s, 0, 0, 0)),
            per_seq,
            per_seq,
            per_seq,
            per_seq,
            pl.BlockSpec((1, 1, bias.shape[2]), lambda s, h: (s, 0, 0)),
        ],
        out_specs=per_head,
        scratch_shapes=[pltpu.VMEM((NEW, HD), jnp.bfloat16)],
        compiler_params=pltpu.CompilerParams(vmem_limit_bytes=48 * 2**20),
        name="attention",
    )(query, old, key_raw, value, cosine, sine, bias)


def output_phases(
    order, greet, mixture, weight, destination, result,
    everyone, weight_all, outgoing, incoming,
    weight_sem, send_sem, recv_sem, swap_send, swap_recv,
):
    position, index = order
    n = incoming.shape[0]
    half, part = incoming.shape[3], incoming.shape[4]
    width = 2 * part
    me = lax.axis_index("tensor")
    worker = lax.axis_index("worker")
    workers = everyone.shape[0]
    place = position(me)
    forward = index(lax.rem(place + 1, n))
    back = index(lax.rem(place + n - 1, n))
    targets = (forward, back)

    def weight_copy(block):
        cols = pl.ds(pl.multiple_of(block * width, width), width)
        return pltpu.make_async_copy(
            weight.at[:, cols], weight_all.at[block], weight_sem.at[block]
        )

    def start_weights(k, carry):
        weight_copy(index(lax.rem(place + n - 1 - k, n))).start()

        @pl.when(k < n // 2 - 1)
        def _():
            weight_copy(index(lax.rem(place + 1 + k, n))).start()

        return carry

    def begin():
        if greet:
            barrier = pltpu.get_barrier_semaphore()
            for target in targets:
                pl.semaphore_signal(
                    barrier, inc=1, device_id={"tensor": target}, device_id_type=MESH
                )
            for k in range(1, workers):
                pl.semaphore_signal(
                    barrier,
                    inc=1,
                    device_id={"worker": lax.rem(worker + k, workers)},
                    device_id_type=MESH,
                )
        lax.fori_loop(0, n // 2, start_weights, 0)
        weight_copy(me).start()
        for r in range(2):
            for d in range(2):
                incoming[0, r, d] = jnp.zeros((half, part), jnp.bfloat16)
        if greet:
            pl.semaphore_wait(barrier, 1 + workers)

    def hop(step, r, d):
        return pltpu.make_async_remote_copy(
            src_ref=outgoing.at[step, r, d],
            dst_ref=incoming.at[step + 1, r, d],
            send_sem=send_sem.at[step, r, d],
            recv_sem=recv_sem.at[step + 1, r, d],
            device_id={"tensor": targets[d]},
            device_id_type=MESH,
        )

    def arrival(step, r, d):
        return pltpu.make_async_remote_copy(
            src_ref=outgoing.at[step, r, d],
            dst_ref=incoming.at[step, r, d],
            send_sem=send_sem.at[step, r, d],
            recv_sem=recv_sem.at[step, r, d],
            device_id={"tensor": targets[d]},
            device_id_type=MESH,
        )

    def add_up(step, r):
        blocks = (
            index(lax.rem(place + 2 * n - 1 - step, n)),
            index(lax.rem(place + 1 + step, n)),
        )

        if r == 0:

            @pl.when(step < n // 2)
            def _():
                weight_copy(blocks[0]).wait()

            @pl.when(step < n // 2 - 1)
            def _():
                weight_copy(blocks[1]).wait()

            @pl.when(step == n // 2)
            def _():
                weight_copy(me).wait()

        for d in range(2):
            product = jnp.dot(
                mixture[r * half : (r + 1) * half, :],
                weight_all[blocks[d], :, d * part : (d + 1) * part],
                preferred_element_type=jnp.float32,
            )

            @pl.when(step > 0)
            def _():
                arrival(step, r, d).wait_recv()

            summed = product + incoming[step, r, d].astype(jnp.float32)
            outgoing[step, r, d] = summed.astype(jnp.bfloat16)

            @pl.when(step < n - 1)
            def _():
                hop(step, r, d).start()

    def swap(k, r):
        return pltpu.make_async_remote_copy(
            src_ref=everyone.at[worker, pl.ds(r * half, half)],
            dst_ref=everyone.at[worker, pl.ds(r * half, half)],
            send_sem=swap_send.at[k, r],
            recv_sem=swap_recv.at[k, r],
            device_id={"worker": lax.rem(worker + k, workers)},
            device_id_type=MESH,
        )

    def hand_over(r):
        for d in range(2):
            everyone[worker, r * half : (r + 1) * half, d * part : (d + 1) * part] = outgoing[
                n - 1, r, d
            ]
        for k in range(1, workers):
            swap(k, r).start()

    def sums():
        def step_body(step, carry):
            add_up(step + 1, 0)
            add_up(step, 1)
            return carry

        lax.fori_loop(0, n - 1, step_body, 0)
        hand_over(0)
        add_up(n - 1, 1)
        hand_over(1)

    def end():
        def finish(step, carry):
            for r in range(2):
                for d in range(2):
                    hop(step, r, d).wait_send()
            return carry

        lax.fori_loop(0, n - 1, finish, 0)
        for r in range(2):
            for k in range(1, workers):
                swap(k, r).wait()

        seqs = destination.shape[0]
        local_seqs = seqs // workers
        bound = [jnp.where(destination[seq] == worker, 1, 0) for seq in range(seqs)]
        rank, ranks = 0, []
        for seq in range(seqs):
            ranks.append(rank)
            rank = rank + bound[seq]
        for slot in range(result.shape[0]):
            chosen = [jnp.where(ranks[seq] == slot, bound[seq], 0) for seq in range(seqs)]
            picked = jnp.zeros(result.shape[1:], result.dtype)
            for seq in range(seqs):
                first = seq % local_seqs * NEW
                rows = everyone[seq // local_seqs, first : first + NEW, :]
                flag = jnp.full(result.shape[1:], chosen[seq], jnp.int32)
                picked = jnp.where(flag > 0, rows, picked)
            result[slot] = picked

    return begin, add_up, sums, end


def output_kernel(order, *refs):
    begin, add_up, sums, end = output_phases(order, True, *refs)
    begin()
    add_up(0, 0)
    sums()
    end()


def output_scratch(n, workers, rows, depth, width):
    half, part = rows // 2, width // 2
    return [
        pltpu.VMEM((workers, rows, width), jnp.bfloat16),
        pltpu.VMEM((n, depth, width), jnp.bfloat16),
        pltpu.VMEM((n, 2, 2, half, part), jnp.bfloat16),
        pltpu.VMEM((n, 2, 2, half, part), jnp.bfloat16),
        pltpu.SemaphoreType.DMA((n,)),
        pltpu.SemaphoreType.DMA((n, 2, 2)),
        pltpu.SemaphoreType.DMA((n, 2, 2)),
        pltpu.SemaphoreType.DMA((workers, 2)),
        pltpu.SemaphoreType.DMA((workers, 2)),
    ]


def project_out(order, n, workers, mixture, weight, destination):
    rows, depth = mixture.shape
    width = weight.shape[1] // n
    vmem = pl.BlockSpec(memory_space=pltpu.VMEM)
    return pl.pallas_call(
        functools.partial(output_kernel, order),
        out_shape=jax.ShapeDtypeStruct((CAP, NEW, width), jnp.bfloat16),
        in_specs=[
            vmem,
            pl.BlockSpec(memory_space=pl.ANY),
            pl.BlockSpec(memory_space=pltpu.SMEM),
        ],
        out_specs=vmem,
        scratch_shapes=output_scratch(n, workers, rows, depth, width),
        compiler_params=pltpu.CompilerParams(
            collective_id=1, has_side_effects=True, vmem_limit_bytes=48 * 2**20
        ),
        name="project_out",
    )(mixture, weight, destination)


def layer_kernel(
    order, grid, seqs, scratch_counts,
    tok, gain, inverse, lengths, wq, wk, wv, cached, bias, weight, destination, result,
    query, key_raw, value, cosine, sine, ctx, mixture, *scratch,
):
    first = scratch_counts
    begin, add_up, sums, end = output_phases(
        order, False, mixture, weight, destination, result, *scratch[first:]
    )
    project_kernel(
        grid, seqs, True, begin, tok, gain, inverse, lengths, wq, wk, wv, cached,
        query, key_raw, value, cosine, sine, ctx, *scratch[:first],
    )
    worker = lax.axis_index("worker")
    count = ctx.shape[0] * ctx.shape[3]
    heads = query.shape[1] // HD
    together = math.gcd(heads, 4)

    def attend(seq):
        lines = slice(seq * NEW, (seq + 1) * NEW)
        raw = key_raw[lines, :].astype(jnp.float32)
        turned = pltpu.roll(raw, HD // 2, 1)
        key = (raw * cosine[lines, :] + turned * sine[lines, :]).astype(jnp.bfloat16)
        key_raw[lines, :] = key

        def some(number, carry):
            attend_heads(
                query,
                ctx[:, seq, 0].reshape(count, HD),
                ctx[:, seq, 1].reshape(count, HD),
                key_raw[lines, :],
                value[lines, :],
                bias[worker * seqs + seq] > 0,
                mixture,
                [
                    pl.ds(pl.multiple_of((number * together + k) * HD, HD), HD)
                    for k in range(together)
                ],
                lines,
            )
            return carry

        lax.fori_loop(0, heads // together, some, 0)

    for seq in range(seqs // 2):
        attend(seq)
    add_up(0, 0)
    for seq in range(seqs // 2, seqs):
        attend(seq)
    sums()
    end()


def layer(order, grid, n, workers, tokens, gain, inverse, lengths, wq, wk, wv, cached, bias, weight, destination):
    rows = tokens.shape[0]
    cols, narrow = wq.shape[1], wk.shape[1]
    width = weight.shape[1] // n
    seqs, stored = cached.shape[0], cached.shape[1]
    vmem = pl.BlockSpec(memory_space=pltpu.VMEM)
    smem = pl.BlockSpec(memory_space=pltpu.SMEM)
    anywhere = pl.BlockSpec(memory_space=pl.ANY)
    scratch = project_scratch(grid, n, tokens, gain, wq, wk, cached)
    return pl.pallas_call(
        functools.partial(layer_kernel, order, grid, seqs, len(scratch)),
        out_shape=jax.ShapeDtypeStruct((CAP, NEW, width), jnp.bfloat16),
        in_specs=[anywhere, anywhere, vmem, smem] + [anywhere] * 4 + [vmem, anywhere, smem],
        out_specs=vmem,
        scratch_shapes=[
            pltpu.VMEM((rows, cols), jnp.bfloat16),
            pltpu.VMEM((rows, narrow), jnp.bfloat16),
            pltpu.VMEM((rows, narrow), jnp.bfloat16),
            pltpu.VMEM((rows, HD), jnp.float32),
            pltpu.VMEM((rows, HD), jnp.float32),
            pltpu.VMEM((n, seqs, 2, stored, HD), jnp.bfloat16),
            pltpu.VMEM((rows, cols), jnp.bfloat16),
        ]
        + scratch
        + output_scratch(n, workers, rows, cols, width),
        compiler_params=pltpu.CompilerParams(
            collective_id=2, has_side_effects=True, vmem_limit_bytes=62 * 2**20
        ),
        name="layer",
    )(tokens, gain, inverse, lengths, wq, wk, wv, cached, bias, weight, destination)


def from_partner(block, axis, bit):
    count = lax.axis_size(axis)
    route = []
    for low in range(count):
        high = low | 1 << bit
        if high != low and high < count:
            route += [(low, high), (high, low)]
    return lax.ppermute(block, axis, route)


def whole_head(block, bits):
    me = lax.axis_index("tensor")
    for bit in range(bits):
        other = from_partner(block, "tensor", bit)
        upper = me // (1 << bit) % 2 == 1
        block = jnp.where(
            upper,
            jnp.concatenate([other, block], axis=1),
            jnp.concatenate([block, other], axis=1),
        )
    return block


def local(
    ring,
    grid,
    tokens,
    norm_gain,
    query_weight,
    key_weight,
    value_weight,
    output_weight,
    cached_blocks,
    cache_length,
    block_table,
    destination,
):
    n = lax.axis_size("tensor")
    workers = lax.axis_size("worker")
    seqs = cached_blocks.shape[0]
    logical = block_table[:, :, None] * BLK + jnp.arange(BLK, dtype=jnp.int32)[None, None, :]
    seen = (logical < cache_length[:, None, None]).astype(jnp.float32)
    seen = seen.reshape(cache_length.shape[0], 1, -1)
    half = 500000.0 ** (-(np.arange(HD // 2) * 2.0 / HD))
    inverse = jnp.asarray(np.concatenate([half, half])[None, :], jnp.float32)
    gain = norm_gain[None, :]
    bits = (n // KVH).bit_length() - 1
    if bits == 0:
        return layer(
            ring, grid, n, workers, tokens, gain, inverse, cache_length,
            query_weight, key_weight, value_weight, cached_blocks, seen,
            output_weight, destination,
        )[None]
    query, key_raw, value, cosine, sine, old = project(
        grid, n, tokens, gain, inverse, cache_length,
        query_weight, key_weight, value_weight, cached_blocks,
    )
    key_raw, value = whole_head(key_raw, bits), whole_head(value, bits)
    seen = lax.dynamic_slice_in_dim(seen, lax.axis_index("worker") * seqs, seqs, 0)
    mixture = attention(query, old, key_raw, value, cosine, sine, seen)
    return project_out(ring, n, workers, mixture, output_weight, destination)[None]


def solution(mesh):
    placed = (
        P(("groups", "worker"), "tensor"),
        P(),
        P(None, "tensor"),
        P(None, "tensor"),
        P(None, "tensor"),
        P("tensor", None),
        P(("groups", "worker"), "tensor", None, None),
        P("groups"),
        P("groups", None),
        P("groups"),
    )
    return jax.shard_map(
        functools.partial(local, *layout(mesh)),
        mesh=mesh,
        in_specs=placed,
        out_specs=P(("groups", "worker"), None, None, "tensor"),
        check_vma=False,
    )
```

```python
import functools
import math

import jax
import jax.numpy as jnp
import numpy as np
from jax import lax
from jax.experimental import pallas as pl
from jax.experimental.pallas import tpu as pltpu
from jax.sharding import PartitionSpec as P

HD = 128
NEW = 128
BLK = 16
CAP = 3
KVH = 8

MESH = pl.DeviceIdType.MESH
epsilon = 1e-05


def snake_order(count):
    def position(index):
        column, row = lax.rem(index, 2), lax.div(index, 2)
        return row + column * (count - 1 - 2 * row)

    def index(place):
        second = lax.div(place, count // 2)
        return second * (2 * (count - 1 - place) + 1) + (1 - second) * (2 * place)

    return position, index


def layout(mesh):
    devices = mesh.devices[0, 0]
    count = devices.shape[0]
    places = [getattr(device, "coords", None) for device in devices]
    if count > 2 and count % 2 == 0 and all(place is not None for place in places):
        ring = list(range(0, count, 2)) + list(range(count - 1, 0, -2))
        steps = [
            sum(abs(a - b) for a, b in zip(places[ring[k]], places[ring[(k + 1) % count]]))
            for k in range(count)
        ]
        if max(steps) == 1:
            return snake_order(count), (count // 2, 2, False)
    return ((lambda index: index), (lambda place: place)), (count, 1, True)


def project_kernel(
    grid, seqs, greet_workers, after_weights, tok, gain_hbm, inverse, lengths, wq, wk, wv, cached,
    q_out, k_out, v_out, cosine, sine, ctx,
    xg, gain, raw, kvt, wq_all, wk_all, wv_all, qacc, kacc, vacc, squares,
    weight_sem, send_sem, recv_sem, old_send, old_recv, own_sem, load_sem,
):
    lines, columns, wraps = grid
    n, parts, rows, part = xg.shape
    width = parts * part
    share = n // kvt.shape[0]
    me = lax.axis_index("tensor")
    worker = lax.axis_index("worker")
    line, column = lax.div(me, columns), lax.rem(me, columns)
    other = columns - 1 - column
    reach = lines // 2 + 1 if wraps else lines

    def source(k, side, where):
        moved = line + lines + (2 * side - 1) * k
        return lax.rem(moved, lines) * columns + where

    def comes(k, side):
        if wraps:
            return k + side <= lines // 2
        from_below = (1 - side) * (line - k)
        from_above = side * (lines - 1 - line - k)
        return from_below + from_above >= 0

    def goes_on(k, side):
        if wraps:
            return k + side < lines // 2
        return (1 - side) * (lines - 1 - line) + side * line > 0

    def neighbour(side):
        return lax.rem(line + lines + 1 - 2 * side, lines) * columns + column

    across = line * columns + other

    def weight_copies(block):
        span = pl.ds(pl.multiple_of(block * width, width), width)
        return [
            pltpu.make_async_copy(src.at[span, :], dst.at[block], weight_sem.at[block, k])
            for k, (src, dst) in enumerate(((wq, wq_all), (wk, wk_all), (wv, wv_all)))
        ]

    def start_weights(block):
        for copy in weight_copies(block):
            copy.start()

    barrier = pltpu.get_barrier_semaphore()

    def greet(k, carry):
        pl.semaphore_signal(
            barrier, inc=1, device_id={"tensor": lax.rem(me + k, n)}, device_id_type=MESH
        )
        return carry

    lax.fori_loop(1, n, greet, 0)
    workers = lax.axis_size("worker") if greet_workers else 1
    for k in range(1, workers):
        pl.semaphore_signal(
            barrier,
            inc=1,
            device_id={"worker": lax.rem(worker + k, workers)},
            device_id_type=MESH,
        )

    def own_part(c):
        span = pl.ds(pl.multiple_of(c * part, part), part)
        return tok.at[:, span]

    own_parts = [
        pltpu.make_async_copy(own_part(c), xg.at[me, c], load_sem.at[c]) for c in range(parts)
    ]
    for copy in own_parts:
        copy.start()
    load_gain = pltpu.make_async_copy(gain_hbm, gain, load_sem.at[parts])
    load_gain.start()
    load_cached = pltpu.make_async_copy(cached, raw, load_sem.at[parts + 1])
    load_cached.start()
    start_weights(me)

    def spread(k, carry):
        for side in range(2):

            @pl.when(comes(k, side))
            def _():
                start_weights(source(k, side, column))

        return carry

    lax.fori_loop(1, reach, spread, 0)
    pl.semaphore_wait(barrier, n - 2 + workers)

    def remote(src, block, c, way, target):
        return pltpu.make_async_remote_copy(
            src_ref=src,
            dst_ref=xg.at[block, c],
            send_sem=send_sem.at[way, block, c],
            recv_sem=recv_sem.at[block, c],
            device_id={"tensor": target},
            device_id_type=MESH,
        )

    def own_hops(c):
        hops = [(goes_on(0, side), remote(own_part(c), me, c, side, neighbour(side))) for side in range(2)]
        if columns > 1:
            hops.append((True, remote(own_part(c), me, c, 2, across)))
        return hops

    for c in range(parts):
        for needed, copy in own_hops(c):
            pl.when(needed)(copy.start)

    def onward(k, side, block, c):
        hops = [(goes_on(k, side), remote(xg.at[block, c], block, c, side, neighbour(side)))]
        if columns > 1:
            hops.append((True, remote(xg.at[block, c], block, c, 2, across)))
        return hops

    def spread_across(k, carry):
        for side in range(2):

            @pl.when(comes(k, side) & (k + 1 > side))
            def _():
                start_weights(source(k, side, other))

        return carry

    if columns > 1:
        start_weights(across)
        lax.fori_loop(1, reach, spread_across, 0)
    if after_weights is not None:
        after_weights()

    units = kvt.shape[0] * raw.shape[0]
    per_piece = -(-units // (2 * parts * (reach - 1)))

    def reorder(unit):
        @pl.when(unit < units)
        def _():
            head, seq = lax.div(unit, raw.shape[0]), lax.rem(unit, raw.shape[0])
            span = pl.ds(pl.multiple_of(head * HD, HD), HD)
            for kind in range(2):
                kvt[head, seq, kind] = raw[seq, :, kind, span]

    def stored(k):
        target = lax.rem(me + k, n)
        return pltpu.make_async_remote_copy(
            src_ref=kvt.at[lax.div(target, share)],
            dst_ref=ctx.at[me],
            send_sem=old_send.at[k],
            recv_sem=old_recv.at[k],
            device_id={"tensor": target},
            device_id_type=MESH,
        )

    def stored_arrival(k):
        origin = lax.rem(me + n - k, n)
        return pltpu.make_async_remote_copy(
            src_ref=kvt.at[0],
            dst_ref=ctx.at[origin],
            send_sem=old_send.at[k],
            recv_sem=old_recv.at[k],
            device_id={"tensor": origin},
            device_id_type=MESH,
        )

    def send_stored(k, carry):
        stored(k).start()
        return carry

    qacc[...] = jnp.zeros_like(qacc)
    kacc[...] = jnp.zeros_like(kacc)
    vacc[...] = jnp.zeros_like(vacc)
    squares[...] = jnp.zeros_like(squares)

    def multiply(block, c):
        @pl.when(c == 0)
        def _():
            for copy in weight_copies(block):
                copy.wait()

        values = xg[block, c].astype(jnp.float32)
        squares[...] += jnp.sum(values * values, axis=1, keepdims=True)
        offset = pl.multiple_of(block * width + c * part, part)
        scaled = (values * gain[:, pl.ds(offset, part)]).astype(jnp.bfloat16)
        span = pl.ds(pl.multiple_of(c * part, part), part)
        for total, weight in ((qacc, wq_all), (kacc, wk_all), (vacc, wv_all)):
            total[...] += jnp.dot(
                scaled, weight[block, span, :], preferred_element_type=jnp.float32
            )

    load_gain.wait()
    load_cached.wait()
    for copy in own_parts:
        copy.wait()

    def own_body(c, carry):
        multiply(me, c)
        return carry

    lax.fori_loop(0, parts, own_body, 0)

    def arrive(block, c):
        remote(xg.at[block, c], block, c, 0, across).wait_recv()

    def along(k, carry):
        def piece(number, carry):
            c, side = lax.div(number, 2), lax.rem(number, 2)
            block = source(k, side, column)

            @pl.when(comes(k, side))
            def _():
                arrive(block, c)
                for needed, copy in onward(k, side, block, c):
                    pl.when(needed)(copy.start)
                multiply(block, c)

            for extra in range(per_piece):
                reorder(((k - 1) * 2 * parts + number) * per_piece + extra)
            return carry

        return lax.fori_loop(0, 2 * parts, piece, carry)

    lax.fori_loop(1, reach, along, 0)
    lax.fori_loop(1, n, send_stored, 0)
    own = pltpu.make_async_copy(kvt.at[lax.div(me, share)], ctx.at[me], own_sem)
    own.start()

    for seq in range(seqs):
        span = slice(seq * NEW, (seq + 1) * NEW)
        start = lengths[worker * seqs + seq]
        position = start + lax.broadcasted_iota(jnp.int32, (NEW, HD), 0)
        angle = position.astype(jnp.float32) * inverse[...]
        lane = lax.broadcasted_iota(jnp.int32, (NEW, HD), 1)
        cosine[span, :] = jnp.cos(angle)
        turn = jnp.sin(angle)
        sine[span, :] = jnp.where(lane < HD // 2, -turn, turn)

    def beyond(k, carry):
        def piece(number, carry):
            c, side = lax.div(number, 2), lax.rem(number, 2)
            block = source(k, side, other)

            @pl.when(comes(k, side) & (k + 1 > side))
            def _():
                arrive(block, c)
                multiply(block, c)

            return carry

        return lax.fori_loop(0, 2 * parts, piece, carry)

    if columns > 1:
        lax.fori_loop(0, reach, beyond, 0)

    factor = lax.rsqrt(squares[...] / (n * width) + epsilon)
    k_out[...] = (kacc[...] * factor).astype(jnp.bfloat16)
    v_out[...] = (vacc[...] * factor).astype(jnp.bfloat16)
    for head in range(q_out.shape[1] // HD):
        cols = slice(head * HD, (head + 1) * HD)
        query = qacc[:, cols] * factor
        turned = pltpu.roll(query, HD // 2, 1)
        q_out[:, cols] = (query * cosine[...] + turned * sine[...]).astype(jnp.bfloat16)

    for c in range(parts):
        for needed, copy in own_hops(c):
            pl.when(needed)(copy.wait_send)

    def sent(k, carry):
        def piece(number, carry):
            c, side = lax.div(number, 2), lax.rem(number, 2)
            block = source(k, side, column)

            @pl.when(comes(k, side))
            def _():
                for needed, copy in onward(k, side, block, c):
                    pl.when(needed)(copy.wait_send)

            return carry

        return lax.fori_loop(0, 2 * parts, piece, carry)

    lax.fori_loop(1, reach, sent, 0)

    def finish(k, carry):
        stored(k).wait_send()
        stored_arrival(k).wait_recv()
        return carry

    lax.fori_loop(1, n, finish, 0)
    own.wait()


def project_scratch(grid, n, tokens, gain, wq, wk, cached):
    rows, width = tokens.shape
    part = max(HD, width // 4)
    parts = width // part
    cols, narrow = wq.shape[1], wk.shape[1]
    ways = 2 + (grid[1] > 1)
    return [
        pltpu.VMEM((n, parts, rows, part), jnp.bfloat16),
        pltpu.VMEM(gain.shape, jnp.float32),
        pltpu.VMEM(cached.shape, jnp.bfloat16),
        pltpu.VMEM((KVH, cached.shape[0], 2, cached.shape[1], HD), jnp.bfloat16),
        pltpu.VMEM((n, width, cols), jnp.bfloat16),
        pltpu.VMEM((n, width, narrow), jnp.bfloat16),
        pltpu.VMEM((n, width, narrow), jnp.bfloat16),
        pltpu.VMEM((rows, cols), jnp.float32),
        pltpu.VMEM((rows, narrow), jnp.float32),
        pltpu.VMEM((rows, narrow), jnp.float32),
        pltpu.VMEM((rows, 1), jnp.float32),
        pltpu.SemaphoreType.DMA((n, 3)),
        pltpu.SemaphoreType.DMA((ways, n, parts)),
        pltpu.SemaphoreType.DMA((n, parts)),
        pltpu.SemaphoreType.DMA((n,)),
        pltpu.SemaphoreType.DMA((n,)),
        pltpu.SemaphoreType.DMA,
        pltpu.SemaphoreType.DMA((parts + 2,)),
    ]


def project(grid, n, tokens, gain, inverse, lengths, wq, wk, wv, cached):
    rows = tokens.shape[0]
    cols, narrow = wq.shape[1], wk.shape[1]
    seqs, stored = cached.shape[0], cached.shape[1]
    vmem = pl.BlockSpec(memory_space=pltpu.VMEM)
    smem = pl.BlockSpec(memory_space=pltpu.SMEM)
    anywhere = pl.BlockSpec(memory_space=pl.ANY)
    return pl.pallas_call(
        functools.partial(project_kernel, grid, seqs, False, None),
        out_shape=(
            jax.ShapeDtypeStruct((rows, cols), jnp.bfloat16),
            jax.ShapeDtypeStruct((rows, narrow), jnp.bfloat16),
            jax.ShapeDtypeStruct((rows, narrow), jnp.bfloat16),
            jax.ShapeDtypeStruct((rows, HD), jnp.float32),
            jax.ShapeDtypeStruct((rows, HD), jnp.float32),
            jax.ShapeDtypeStruct((n, seqs, 2, stored, HD), jnp.bfloat16),
        ),
        in_specs=[anywhere, anywhere, vmem, smem] + [anywhere] * 4,
        out_specs=(vmem,) * 5 + (anywhere,),
        scratch_shapes=project_scratch(grid, n, tokens, gain, wq, wk, cached),
        compiler_params=pltpu.CompilerParams(
            collective_id=0, has_side_effects=True, vmem_limit_bytes=60 * 2**20
        ),
        name="gather_project",
    )(tokens, gain, inverse, lengths, wq, wk, wv, cached)


def attend_heads(query, old_key, old_value, key, value, seen, mixture, heads, lines):
    scale = math.log2(math.e) / math.sqrt(HD)
    contract = (((1,), (1,)), ((), ()))
    row = lax.broadcasted_iota(jnp.int32, (NEW, NEW), 0)
    col = lax.broadcasted_iota(jnp.int32, (NEW, NEW), 1)
    for cols in heads:
        one = query[lines, cols]
        old_scores = lax.dot_general(one, old_key, contract, preferred_element_type=jnp.float32)
        new_scores = lax.dot_general(one, key, contract, preferred_element_type=jnp.float32)
        old_scores = jnp.where(seen, old_scores * scale, -1e30)
        new_scores = jnp.where(row >= col, new_scores * scale, -1e30)
        largest = jnp.maximum(
            jnp.max(old_scores, axis=1, keepdims=True),
            jnp.max(new_scores, axis=1, keepdims=True),
        )
        old_expo = jnp.exp2(old_scores - largest)
        new_expo = jnp.exp2(new_scores - largest)
        inverse = 1.0 / (
            jnp.sum(old_expo, axis=1, keepdims=True) + jnp.sum(new_expo, axis=1, keepdims=True)
        )
        old_probs = (old_expo * inverse).astype(jnp.bfloat16)
        new_probs = (new_expo * inverse).astype(jnp.bfloat16)
        mixed = jnp.dot(old_probs, old_value, preferred_element_type=jnp.float32)
        mixed += jnp.dot(new_probs, value, preferred_element_type=jnp.float32)
        mixture[lines, cols] = mixed.astype(jnp.bfloat16)


def attend_kernel(query, old, key_raw, value, cosine, sine, bias, mixture, key_turned):
    @pl.when(pl.program_id(1) == 0)
    def _():
        raw = key_raw[...].astype(jnp.float32)
        turned = pltpu.roll(raw, HD // 2, 1)
        key_turned[...] = (raw * cosine[...] + turned * sine[...]).astype(jnp.bfloat16)

    count = old.shape[0] * old.shape[3]
    attend_heads(
        query,
        old[:, 0, 0].reshape(count, HD),
        old[:, 0, 1].reshape(count, HD),
        key_turned[...],
        value[...],
        bias[0] > 0,
        mixture,
        [slice(head * HD, (head + 1) * HD) for head in range(query.shape[1] // HD)],
        slice(None),
    )


def attention(query, old, key_raw, value, cosine, sine, bias):
    seqs = old.shape[1]
    heads = query.shape[1] // HD
    together = math.gcd(heads, 4)
    per_seq = pl.BlockSpec((NEW, HD), lambda s, h: (s, 0))
    per_head = pl.BlockSpec((NEW, HD * together), lambda s, h: (s, h))
    return pl.pallas_call(
        attend_kernel,
        out_shape=jax.ShapeDtypeStruct(query.shape, jnp.bfloat16),
        grid=(seqs, heads // together),
        in_specs=[
            per_head,
            pl.BlockSpec((old.shape[0], 1) + old.shape[2:], lambda s, h: (0, s, 0, 0, 0)),
            per_seq,
            per_seq,
            per_seq,
            per_seq,
            pl.BlockSpec((1, 1, bias.shape[2]), lambda s, h: (s, 0, 0)),
        ],
        out_specs=per_head,
        scratch_shapes=[pltpu.VMEM((NEW, HD), jnp.bfloat16)],
        compiler_params=pltpu.CompilerParams(vmem_limit_bytes=48 * 2**20),
        name="attention",
    )(query, old, key_raw, value, cosine, sine, bias)


def output_phases(
    order, greet, mixture, weight, destination, result,
    everyone, weight_all, incoming,
    weight_sem, send_sem, recv_sem, swap_send, swap_recv,
):
    position, index = order
    n = incoming.shape[0]
    half, part = incoming.shape[3], incoming.shape[4]
    width = 2 * part
    me = lax.axis_index("tensor")
    worker = lax.axis_index("worker")
    workers = everyone.shape[0]
    place = position(me)
    forward = index(lax.rem(place + 1, n))
    back = index(lax.rem(place + n - 1, n))
    targets = (forward, back)

    def weight_copy(block):
        cols = pl.ds(pl.multiple_of(block * width, width), width)
        return pltpu.make_async_copy(
            weight.at[:, cols], weight_all.at[block], weight_sem.at[block]
        )

    def start_weights(k, carry):
        weight_copy(index(lax.rem(place + n - 1 - k, n))).start()

        @pl.when(k < n // 2 - 1)
        def _():
            weight_copy(index(lax.rem(place + 1 + k, n))).start()

        return carry

    def begin():
        if greet:
            barrier = pltpu.get_barrier_semaphore()
            for target in targets:
                pl.semaphore_signal(
                    barrier, inc=1, device_id={"tensor": target}, device_id_type=MESH
                )
            for k in range(1, workers):
                pl.semaphore_signal(
                    barrier,
                    inc=1,
                    device_id={"worker": lax.rem(worker + k, workers)},
                    device_id_type=MESH,
                )
        lax.fori_loop(0, n // 2, start_weights, 0)
        weight_copy(me).start()
        for r in range(2):
            for d in range(2):
                incoming[0, r, d] = jnp.zeros((half, part), jnp.bfloat16)
        if greet:
            pl.semaphore_wait(barrier, 1 + workers)

    def hop(step, r, d):
        return pltpu.make_async_remote_copy(
            src_ref=incoming.at[step, r, d],
            dst_ref=incoming.at[step + 1, r, d],
            send_sem=send_sem.at[step, r, d],
            recv_sem=recv_sem.at[step + 1, r, d],
            device_id={"tensor": targets[d]},
            device_id_type=MESH,
        )

    def arrival(step, r, d):
        return pltpu.make_async_remote_copy(
            src_ref=incoming.at[step, r, d],
            dst_ref=incoming.at[step, r, d],
            send_sem=send_sem.at[step, r, d],
            recv_sem=recv_sem.at[step, r, d],
            device_id={"tensor": targets[d]},
            device_id_type=MESH,
        )

    def add_up(step, r):
        blocks = (
            index(lax.rem(place + 2 * n - 1 - step, n)),
            index(lax.rem(place + 1 + step, n)),
        )

        if r == 0:

            @pl.when(step < n // 2)
            def _():
                weight_copy(blocks[0]).wait()

            @pl.when(step < n // 2 - 1)
            def _():
                weight_copy(blocks[1]).wait()

            @pl.when(step == n // 2)
            def _():
                weight_copy(me).wait()

        for d in range(2):
            product = jnp.dot(
                mixture[r * half : (r + 1) * half, :],
                weight_all[blocks[d], :, d * part : (d + 1) * part],
                preferred_element_type=jnp.float32,
            )

            @pl.when(step > 0)
            def _():
                arrival(step, r, d).wait_recv()

            summed = product + incoming[step, r, d].astype(jnp.float32)
            incoming[step, r, d] = summed.astype(jnp.bfloat16)

            @pl.when(step < n - 1)
            def _():
                hop(step, r, d).start()

    def swap(k, r):
        return pltpu.make_async_remote_copy(
            src_ref=everyone.at[worker, pl.ds(r * half, half)],
            dst_ref=everyone.at[worker, pl.ds(r * half, half)],
            send_sem=swap_send.at[k, r],
            recv_sem=swap_recv.at[k, r],
            device_id={"worker": lax.rem(worker + k, workers)},
            device_id_type=MESH,
        )

    def hand_over(r):
        for d in range(2):
            everyone[worker, r * half : (r + 1) * half, d * part : (d + 1) * part] = incoming[
                n - 1, r, d
            ]
        for k in range(1, workers):
            swap(k, r).start()

    def sums():
        def step_body(step, carry):
            add_up(step + 1, 0)
            add_up(step, 1)
            return carry

        lax.fori_loop(0, n - 1, step_body, 0)
        hand_over(0)
        add_up(n - 1, 1)
        hand_over(1)

    def end():
        def finish(step, carry):
            for r in range(2):
                for d in range(2):
                    hop(step, r, d).wait_send()
            return carry

        lax.fori_loop(0, n - 1, finish, 0)
        for r in range(2):
            for k in range(1, workers):
                swap(k, r).wait()

        seqs = destination.shape[0]
        local_seqs = seqs // workers
        bound = [jnp.where(destination[seq] == worker, 1, 0) for seq in range(seqs)]
        rank, ranks = 0, []
        for seq in range(seqs):
            ranks.append(rank)
            rank = rank + bound[seq]
        for slot in range(result.shape[0]):
            chosen = [jnp.where(ranks[seq] == slot, bound[seq], 0) for seq in range(seqs)]
            picked = jnp.zeros(result.shape[1:], result.dtype)
            for seq in range(seqs):
                first = seq % local_seqs * NEW
                rows = everyone[seq // local_seqs, first : first + NEW, :]
                flag = jnp.full(result.shape[1:], chosen[seq], jnp.int32)
                picked = jnp.where(flag > 0, rows, picked)
            result[slot] = picked

    return begin, add_up, sums, end


def output_kernel(order, *refs):
    begin, add_up, sums, end = output_phases(order, True, *refs)
    begin()
    add_up(0, 0)
    sums()
    end()


def output_scratch(n, workers, rows, depth, width):
    half, part = rows // 2, width // 2
    return [
        pltpu.VMEM((workers, rows, width), jnp.bfloat16),
        pltpu.VMEM((n, depth, width), jnp.bfloat16),
        pltpu.VMEM((n, 2, 2, half, part), jnp.bfloat16),
        pltpu.SemaphoreType.DMA((n,)),
        pltpu.SemaphoreType.DMA((n, 2, 2)),
        pltpu.SemaphoreType.DMA((n, 2, 2)),
        pltpu.SemaphoreType.DMA((workers, 2)),
        pltpu.SemaphoreType.DMA((workers, 2)),
    ]


def project_out(order, n, workers, mixture, weight, destination):
    rows, depth = mixture.shape
    width = weight.shape[1] // n
    vmem = pl.BlockSpec(memory_space=pltpu.VMEM)
    return pl.pallas_call(
        functools.partial(output_kernel, order),
        out_shape=jax.ShapeDtypeStruct((CAP, NEW, width), jnp.bfloat16),
        in_specs=[
            vmem,
            pl.BlockSpec(memory_space=pl.ANY),
            pl.BlockSpec(memory_space=pltpu.SMEM),
        ],
        out_specs=vmem,
        scratch_shapes=output_scratch(n, workers, rows, depth, width),
        compiler_params=pltpu.CompilerParams(
            collective_id=1, has_side_effects=True, vmem_limit_bytes=48 * 2**20
        ),
        name="project_out",
    )(mixture, weight, destination)


def layer_kernel(
    order, grid, seqs, scratch_counts,
    tok, gain, inverse, lengths, wq, wk, wv, cached, tables, weight, destination, result,
    seen, query, key_raw, value, cosine, sine, ctx, mixture, *scratch,
):
    first = scratch_counts
    begin, add_up, sums, end = output_phases(
        order, False, mixture, weight, destination, result, *scratch[first:]
    )
    project_kernel(
        grid, seqs, True, begin, tok, gain, inverse, lengths, wq, wk, wv, cached,
        query, key_raw, value, cosine, sine, ctx, *scratch[:first],
    )
    worker = lax.axis_index("worker")
    count = ctx.shape[0] * ctx.shape[3]
    heads = query.shape[1] // HD
    together = math.gcd(heads, 4)

    def look(seq):
        row = tables[pl.ds(worker * seqs + seq, 1), :].astype(jnp.float32)
        rows = jnp.broadcast_to(row, (8, row.shape[1])).astype(jnp.bfloat16)
        slot = lax.broadcasted_iota(jnp.int32, (row.shape[1], count), 1)
        block = lax.broadcasted_iota(jnp.int32, (row.shape[1], count), 0)
        pick = jnp.where(lax.div(slot, BLK) == block, 1.0, 0.0).astype(jnp.bfloat16)
        held = jnp.dot(rows, pick, preferred_element_type=jnp.float32)
        inside = lax.broadcasted_iota(jnp.int32, held.shape, 1)
        logical = held.astype(jnp.int32) * BLK + lax.rem(inside, BLK)
        return jnp.where(logical < lengths[worker * seqs + seq], 1.0, 0.0)

    def attend(seq):
        seen[...] = look(seq)
        lines = slice(seq * NEW, (seq + 1) * NEW)
        raw = key_raw[lines, :].astype(jnp.float32)
        turned = pltpu.roll(raw, HD // 2, 1)
        key = (raw * cosine[lines, :] + turned * sine[lines, :]).astype(jnp.bfloat16)
        key_raw[lines, :] = key

        def some(number, carry):
            attend_heads(
                query,
                ctx[:, seq, 0].reshape(count, HD),
                ctx[:, seq, 1].reshape(count, HD),
                key_raw[lines, :],
                value[lines, :],
                seen[0:1, :] > 0,
                mixture,
                [
                    pl.ds(pl.multiple_of((number * together + k) * HD, HD), HD)
                    for k in range(together)
                ],
                lines,
            )
            return carry

        lax.fori_loop(0, heads // together, some, 0)

    for seq in range(seqs // 2):
        attend(seq)
    add_up(0, 0)
    for seq in range(seqs // 2, seqs):
        attend(seq)
    sums()
    end()


def layer(order, grid, n, workers, tokens, gain, inverse, lengths, wq, wk, wv, cached, tables, weight, destination):
    rows = tokens.shape[0]
    cols, narrow = wq.shape[1], wk.shape[1]
    width = weight.shape[1] // n
    seqs, stored = cached.shape[0], cached.shape[1]
    vmem = pl.BlockSpec(memory_space=pltpu.VMEM)
    smem = pl.BlockSpec(memory_space=pltpu.SMEM)
    anywhere = pl.BlockSpec(memory_space=pl.ANY)
    scratch = project_scratch(grid, n, tokens, gain, wq, wk, cached)
    return pl.pallas_call(
        functools.partial(layer_kernel, order, grid, seqs, len(scratch)),
        out_shape=jax.ShapeDtypeStruct((CAP, NEW, width), jnp.bfloat16),
        in_specs=[anywhere, anywhere, vmem, smem] + [anywhere] * 4 + [vmem, anywhere, smem],
        out_specs=vmem,
        scratch_shapes=[
            pltpu.VMEM((8, n * stored), jnp.float32),
            pltpu.VMEM((rows, cols), jnp.bfloat16),
            pltpu.VMEM((rows, narrow), jnp.bfloat16),
            pltpu.VMEM((rows, narrow), jnp.bfloat16),
            pltpu.VMEM((rows, HD), jnp.float32),
            pltpu.VMEM((rows, HD), jnp.float32),
            pltpu.VMEM((n, seqs, 2, stored, HD), jnp.bfloat16),
            pltpu.VMEM((rows, cols), jnp.bfloat16),
        ]
        + scratch
        + output_scratch(n, workers, rows, cols, width),
        compiler_params=pltpu.CompilerParams(
            collective_id=2, has_side_effects=True, vmem_limit_bytes=57 * 2**20
        ),
        name="layer",
    )(tokens, gain, inverse, lengths, wq, wk, wv, cached, tables, weight, destination)


def from_partner(block, axis, bit):
    count = lax.axis_size(axis)
    route = []
    for low in range(count):
        high = low | 1 << bit
        if high != low and high < count:
            route += [(low, high), (high, low)]
    return lax.ppermute(block, axis, route)


def whole_head(block, bits):
    me = lax.axis_index("tensor")
    for bit in range(bits):
        other = from_partner(block, "tensor", bit)
        upper = me // (1 << bit) % 2 == 1
        block = jnp.where(
            upper,
            jnp.concatenate([other, block], axis=1),
            jnp.concatenate([block, other], axis=1),
        )
    return block


def local(
    ring,
    grid,
    tokens,
    norm_gain,
    query_weight,
    key_weight,
    value_weight,
    output_weight,
    cached_blocks,
    cache_length,
    block_table,
    destination,
):
    n = lax.axis_size("tensor")
    workers = lax.axis_size("worker")
    seqs = cached_blocks.shape[0]
    logical = block_table[:, :, None] * BLK + jnp.arange(BLK, dtype=jnp.int32)[None, None, :]
    seen = (logical < cache_length[:, None, None]).astype(jnp.float32)
    seen = seen.reshape(cache_length.shape[0], 1, -1)
    half = 500000.0 ** (-(np.arange(HD // 2) * 2.0 / HD))
    inverse = jnp.asarray(np.concatenate([half, half])[None, :], jnp.float32)
    gain = norm_gain[None, :]
    bits = (n // KVH).bit_length() - 1
    if bits == 0:
        return layer(
            ring, grid, n, workers, tokens, gain, inverse, cache_length,
            query_weight, key_weight, value_weight, cached_blocks, block_table,
            output_weight, destination,
        )[None]
    query, key_raw, value, cosine, sine, old = project(
        grid, n, tokens, gain, inverse, cache_length,
        query_weight, key_weight, value_weight, cached_blocks,
    )
    key_raw, value = whole_head(key_raw, bits), whole_head(value, bits)
    seen = lax.dynamic_slice_in_dim(seen, lax.axis_index("worker") * seqs, seqs, 0)
    mixture = attention(query, old, key_raw, value, cosine, sine, seen)
    return project_out(ring, n, workers, mixture, output_weight, destination)[None]


def solution(mesh):
    placed = (
        P(("groups", "worker"), "tensor"),
        P(),
        P(None, "tensor"),
        P(None, "tensor"),
        P(None, "tensor"),
        P("tensor", None),
        P(("groups", "worker"), "tensor", None, None),
        P("groups"),
        P("groups", None),
        P("groups"),
    )
    return jax.shard_map(
        functools.partial(local, *layout(mesh)),
        mesh=mesh,
        in_specs=placed,
        out_specs=P(("groups", "worker"), None, None, "tensor"),
        check_vma=False,
    )
```

```python
import functools
import math

import jax
import jax.numpy as jnp
import numpy as np
from jax import lax
from jax.experimental import pallas as pl
from jax.experimental.pallas import tpu as pltpu
from jax.sharding import PartitionSpec as P

HD = 128
NEW = 128
BLK = 16
CAP = 3
KVH = 8

MESH = pl.DeviceIdType.MESH
epsilon = 1e-05


def snake_order(count):
    def position(index):
        column, row = lax.rem(index, 2), lax.div(index, 2)
        return row + column * (count - 1 - 2 * row)

    def index(place):
        second = lax.div(place, count // 2)
        return second * (2 * (count - 1 - place) + 1) + (1 - second) * (2 * place)

    return position, index


def layout(mesh):
    devices = mesh.devices[0, 0]
    count = devices.shape[0]
    places = [getattr(device, "coords", None) for device in devices]
    if count > 2 and count % 2 == 0 and all(place is not None for place in places):
        ring = list(range(0, count, 2)) + list(range(count - 1, 0, -2))
        steps = [
            sum(abs(a - b) for a, b in zip(places[ring[k]], places[ring[(k + 1) % count]]))
            for k in range(count)
        ]
        if max(steps) == 1:
            return snake_order(count), (count // 2, 2, False)
    return ((lambda index: index), (lambda place: place)), (count, 1, True)


def project_kernel(
    grid, seqs, greet_workers, after_weights, tok, gain_hbm, inverse, lengths, wq, wk, wv, cached,
    q_out, k_out, v_out, cosine, sine, ctx,
    xg, gain, raw, kvt, wq_all, wk_all, wv_all, qacc, kacc, vacc, squares,
    weight_sem, send_sem, recv_sem, old_send, old_recv, own_sem, load_sem,
):
    lines, columns, wraps = grid
    n, parts, rows, part = xg.shape
    width = parts * part
    share = n // kvt.shape[0]
    me = lax.axis_index("tensor")
    worker = lax.axis_index("worker")
    line, column = lax.div(me, columns), lax.rem(me, columns)
    other = columns - 1 - column
    reach = lines // 2 + 1 if wraps else lines

    def source(k, side, where):
        moved = line + lines + (2 * side - 1) * k
        return lax.rem(moved, lines) * columns + where

    def comes(k, side):
        if wraps:
            return k + side <= lines // 2
        from_below = (1 - side) * (line - k)
        from_above = side * (lines - 1 - line - k)
        return from_below + from_above >= 0

    def goes_on(k, side):
        if wraps:
            return k + side < lines // 2
        return (1 - side) * (lines - 1 - line) + side * line > 0

    def neighbour(side):
        return lax.rem(line + lines + 1 - 2 * side, lines) * columns + column

    across = line * columns + other

    def weight_copies(block):
        span = pl.ds(pl.multiple_of(block * width, width), width)
        return [
            pltpu.make_async_copy(src.at[span, :], dst.at[block], weight_sem.at[block, k])
            for k, (src, dst) in enumerate(((wq, wq_all), (wk, wk_all), (wv, wv_all)))
        ]

    def start_weights(block):
        for copy in weight_copies(block):
            copy.start()

    barrier = pltpu.get_barrier_semaphore()

    def greet(k, carry):
        pl.semaphore_signal(
            barrier, inc=1, device_id={"tensor": lax.rem(me + k, n)}, device_id_type=MESH
        )
        return carry

    lax.fori_loop(1, n, greet, 0)
    workers = lax.axis_size("worker") if greet_workers else 1
    for k in range(1, workers):
        pl.semaphore_signal(
            barrier,
            inc=1,
            device_id={"worker": lax.rem(worker + k, workers)},
            device_id_type=MESH,
        )

    def own_part(c):
        span = pl.ds(pl.multiple_of(c * part, part), part)
        return tok.at[:, span]

    own_parts = [
        pltpu.make_async_copy(own_part(c), xg.at[me, c], load_sem.at[c]) for c in range(parts)
    ]
    for copy in own_parts:
        copy.start()
    load_gain = pltpu.make_async_copy(gain_hbm, gain, load_sem.at[parts])
    load_gain.start()
    load_cached = pltpu.make_async_copy(cached, raw, load_sem.at[parts + 1])
    load_cached.start()
    start_weights(me)

    def spread(k, carry):
        for side in range(2):

            @pl.when(comes(k, side))
            def _():
                start_weights(source(k, side, column))

        return carry

    lax.fori_loop(1, reach, spread, 0)
    pl.semaphore_wait(barrier, n - 2 + workers)

    def remote(src, block, c, way, target):
        return pltpu.make_async_remote_copy(
            src_ref=src,
            dst_ref=xg.at[block, c],
            send_sem=send_sem.at[way, block, c],
            recv_sem=recv_sem.at[block, c],
            device_id={"tensor": target},
            device_id_type=MESH,
        )

    def own_hops(c):
        hops = [(goes_on(0, side), remote(own_part(c), me, c, side, neighbour(side))) for side in range(2)]
        if columns > 1:
            hops.append((True, remote(own_part(c), me, c, 2, across)))
        return hops

    for c in range(parts):
        for needed, copy in own_hops(c):
            pl.when(needed)(copy.start)

    def onward(k, side, block, c):
        hops = [(goes_on(k, side), remote(xg.at[block, c], block, c, side, neighbour(side)))]
        if columns > 1:
            hops.append((True, remote(xg.at[block, c], block, c, 2, across)))
        return hops

    def spread_across(k, carry):
        for side in range(2):

            @pl.when(comes(k, side) & (k + 1 > side))
            def _():
                start_weights(source(k, side, other))

        return carry

    if columns > 1:
        start_weights(across)
        lax.fori_loop(1, reach, spread_across, 0)
    if after_weights is not None:
        after_weights()

    units = kvt.shape[0] * raw.shape[0]
    per_piece = -(-units // (2 * parts))

    def reorder(unit):
        @pl.when(unit < units)
        def _():
            head, seq = lax.div(unit, raw.shape[0]), lax.rem(unit, raw.shape[0])
            span = pl.ds(pl.multiple_of(head * HD, HD), HD)
            for kind in range(2):
                kvt[head, seq, kind] = raw[seq, :, kind, span]

    def stored(k):
        target = lax.rem(me + k, n)
        return pltpu.make_async_remote_copy(
            src_ref=kvt.at[lax.div(target, share)],
            dst_ref=ctx.at[me],
            send_sem=old_send.at[k],
            recv_sem=old_recv.at[k],
            device_id={"tensor": target},
            device_id_type=MESH,
        )

    def stored_arrival(k):
        origin = lax.rem(me + n - k, n)
        return pltpu.make_async_remote_copy(
            src_ref=kvt.at[0],
            dst_ref=ctx.at[origin],
            send_sem=old_send.at[k],
            recv_sem=old_recv.at[k],
            device_id={"tensor": origin},
            device_id_type=MESH,
        )

    def send_stored(k, carry):
        stored(k).start()
        return carry

    qacc[...] = jnp.zeros_like(qacc)
    kacc[...] = jnp.zeros_like(kacc)
    vacc[...] = jnp.zeros_like(vacc)
    squares[...] = jnp.zeros_like(squares)

    def multiply(block, c):
        @pl.when(c == 0)
        def _():
            for copy in weight_copies(block):
                copy.wait()

        values = xg[block, c].astype(jnp.float32)
        squares[...] += jnp.sum(values * values, axis=1, keepdims=True)
        offset = pl.multiple_of(block * width + c * part, part)
        scaled = (values * gain[:, pl.ds(offset, part)]).astype(jnp.bfloat16)
        span = pl.ds(pl.multiple_of(c * part, part), part)
        for total, weight in ((qacc, wq_all), (kacc, wk_all), (vacc, wv_all)):
            total[...] += jnp.dot(
                scaled, weight[block, span, :], preferred_element_type=jnp.float32
            )

    load_gain.wait()
    load_cached.wait()
    for copy in own_parts:
        copy.wait()

    def own_body(c, carry):
        multiply(me, c)
        return carry

    lax.fori_loop(0, parts, own_body, 0)

    def arrive(block, c):
        remote(xg.at[block, c], block, c, 0, across).wait_recv()

    def along(k, carry):
        @pl.when(k == 2)
        def _():
            lax.fori_loop(1, n, send_stored, 0)

        def piece(number, carry):
            c, side = lax.div(number, 2), lax.rem(number, 2)
            block = source(k, side, column)

            @pl.when(comes(k, side))
            def _():
                arrive(block, c)
                for needed, copy in onward(k, side, block, c):
                    pl.when(needed)(copy.start)
                multiply(block, c)

            for extra in range(per_piece):
                reorder(((k - 1) * 2 * parts + number) * per_piece + extra)
            return carry

        return lax.fori_loop(0, 2 * parts, piece, carry)

    lax.fori_loop(1, reach, along, 0)
    own = pltpu.make_async_copy(kvt.at[lax.div(me, share)], ctx.at[me], own_sem)
    own.start()

    for seq in range(seqs):
        span = slice(seq * NEW, (seq + 1) * NEW)
        start = lengths[worker * seqs + seq]
        position = start + lax.broadcasted_iota(jnp.int32, (NEW, HD), 0)
        angle = position.astype(jnp.float32) * inverse[...]
        lane = lax.broadcasted_iota(jnp.int32, (NEW, HD), 1)
        cosine[span, :] = jnp.cos(angle)
        turn = jnp.sin(angle)
        sine[span, :] = jnp.where(lane < HD // 2, -turn, turn)

    def beyond(k, carry):
        def piece(number, carry):
            c, side = lax.div(number, 2), lax.rem(number, 2)
            block = source(k, side, other)

            @pl.when(comes(k, side) & (k + 1 > side))
            def _():
                arrive(block, c)
                multiply(block, c)

            return carry

        return lax.fori_loop(0, 2 * parts, piece, carry)

    if columns > 1:
        lax.fori_loop(0, reach, beyond, 0)

    factor = lax.rsqrt(squares[...] / (n * width) + epsilon)
    k_out[...] = (kacc[...] * factor).astype(jnp.bfloat16)
    v_out[...] = (vacc[...] * factor).astype(jnp.bfloat16)
    for head in range(q_out.shape[1] // HD):
        cols = slice(head * HD, (head + 1) * HD)
        query = qacc[:, cols] * factor
        turned = pltpu.roll(query, HD // 2, 1)
        q_out[:, cols] = (query * cosine[...] + turned * sine[...]).astype(jnp.bfloat16)

    for c in range(parts):
        for needed, copy in own_hops(c):
            pl.when(needed)(copy.wait_send)

    def sent(k, carry):
        def piece(number, carry):
            c, side = lax.div(number, 2), lax.rem(number, 2)
            block = source(k, side, column)

            @pl.when(comes(k, side))
            def _():
                for needed, copy in onward(k, side, block, c):
                    pl.when(needed)(copy.wait_send)

            return carry

        return lax.fori_loop(0, 2 * parts, piece, carry)

    lax.fori_loop(1, reach, sent, 0)

    def finish(k, carry):
        stored(k).wait_send()
        stored_arrival(k).wait_recv()
        return carry

    lax.fori_loop(1, n, finish, 0)
    own.wait()


def project_scratch(grid, n, tokens, gain, wq, wk, cached):
    rows, width = tokens.shape
    part = max(HD, width // 4)
    parts = width // part
    cols, narrow = wq.shape[1], wk.shape[1]
    ways = 2 + (grid[1] > 1)
    return [
        pltpu.VMEM((n, parts, rows, part), jnp.bfloat16),
        pltpu.VMEM(gain.shape, jnp.float32),
        pltpu.VMEM(cached.shape, jnp.bfloat16),
        pltpu.VMEM((KVH, cached.shape[0], 2, cached.shape[1], HD), jnp.bfloat16),
        pltpu.VMEM((n, width, cols), jnp.bfloat16),
        pltpu.VMEM((n, width, narrow), jnp.bfloat16),
        pltpu.VMEM((n, width, narrow), jnp.bfloat16),
        pltpu.VMEM((rows, cols), jnp.float32),
        pltpu.VMEM((rows, narrow), jnp.float32),
        pltpu.VMEM((rows, narrow), jnp.float32),
        pltpu.VMEM((rows, 1), jnp.float32),
        pltpu.SemaphoreType.DMA((n, 3)),
        pltpu.SemaphoreType.DMA((ways, n, parts)),
        pltpu.SemaphoreType.DMA((n, parts)),
        pltpu.SemaphoreType.DMA((n,)),
        pltpu.SemaphoreType.DMA((n,)),
        pltpu.SemaphoreType.DMA,
        pltpu.SemaphoreType.DMA((parts + 2,)),
    ]


def project(grid, n, tokens, gain, inverse, lengths, wq, wk, wv, cached):
    rows = tokens.shape[0]
    cols, narrow = wq.shape[1], wk.shape[1]
    seqs, stored = cached.shape[0], cached.shape[1]
    vmem = pl.BlockSpec(memory_space=pltpu.VMEM)
    smem = pl.BlockSpec(memory_space=pltpu.SMEM)
    anywhere = pl.BlockSpec(memory_space=pl.ANY)
    return pl.pallas_call(
        functools.partial(project_kernel, grid, seqs, False, None),
        out_shape=(
            jax.ShapeDtypeStruct((rows, cols), jnp.bfloat16),
            jax.ShapeDtypeStruct((rows, narrow), jnp.bfloat16),
            jax.ShapeDtypeStruct((rows, narrow), jnp.bfloat16),
            jax.ShapeDtypeStruct((rows, HD), jnp.float32),
            jax.ShapeDtypeStruct((rows, HD), jnp.float32),
            jax.ShapeDtypeStruct((n, seqs, 2, stored, HD), jnp.bfloat16),
        ),
        in_specs=[anywhere, anywhere, vmem, smem] + [anywhere] * 4,
        out_specs=(vmem,) * 5 + (anywhere,),
        scratch_shapes=project_scratch(grid, n, tokens, gain, wq, wk, cached),
        compiler_params=pltpu.CompilerParams(
            collective_id=0, has_side_effects=True, vmem_limit_bytes=60 * 2**20
        ),
        name="gather_project",
    )(tokens, gain, inverse, lengths, wq, wk, wv, cached)


def attend_heads(query, old_key, old_value, key, value, seen, mixture, heads, lines):
    scale = math.log2(math.e) / math.sqrt(HD)
    contract = (((1,), (1,)), ((), ()))
    row = lax.broadcasted_iota(jnp.int32, (NEW, NEW), 0)
    col = lax.broadcasted_iota(jnp.int32, (NEW, NEW), 1)
    for cols in heads:
        one = query[lines, cols]
        old_scores = lax.dot_general(one, old_key, contract, preferred_element_type=jnp.float32)
        new_scores = lax.dot_general(one, key, contract, preferred_element_type=jnp.float32)
        old_scores = jnp.where(seen, old_scores * scale, -1e30)
        new_scores = jnp.where(row >= col, new_scores * scale, -1e30)
        largest = jnp.maximum(
            jnp.max(old_scores, axis=1, keepdims=True),
            jnp.max(new_scores, axis=1, keepdims=True),
        )
        old_expo = jnp.exp2(old_scores - largest)
        new_expo = jnp.exp2(new_scores - largest)
        inverse = 1.0 / (
            jnp.sum(old_expo, axis=1, keepdims=True) + jnp.sum(new_expo, axis=1, keepdims=True)
        )
        old_probs = (old_expo * inverse).astype(jnp.bfloat16)
        new_probs = (new_expo * inverse).astype(jnp.bfloat16)
        mixed = jnp.dot(old_probs, old_value, preferred_element_type=jnp.float32)
        mixed += jnp.dot(new_probs, value, preferred_element_type=jnp.float32)
        mixture[lines, cols] = mixed.astype(jnp.bfloat16)


def attend_kernel(query, old, key_raw, value, cosine, sine, bias, mixture, key_turned):
    @pl.when(pl.program_id(1) == 0)
    def _():
        raw = key_raw[...].astype(jnp.float32)
        turned = pltpu.roll(raw, HD // 2, 1)
        key_turned[...] = (raw * cosine[...] + turned * sine[...]).astype(jnp.bfloat16)

    count = old.shape[0] * old.shape[3]
    attend_heads(
        query,
        old[:, 0, 0].reshape(count, HD),
        old[:, 0, 1].reshape(count, HD),
        key_turned[...],
        value[...],
        bias[0] > 0,
        mixture,
        [slice(head * HD, (head + 1) * HD) for head in range(query.shape[1] // HD)],
        slice(None),
    )


def attention(query, old, key_raw, value, cosine, sine, bias):
    seqs = old.shape[1]
    heads = query.shape[1] // HD
    together = math.gcd(heads, 4)
    per_seq = pl.BlockSpec((NEW, HD), lambda s, h: (s, 0))
    per_head = pl.BlockSpec((NEW, HD * together), lambda s, h: (s, h))
    return pl.pallas_call(
        attend_kernel,
        out_shape=jax.ShapeDtypeStruct(query.shape, jnp.bfloat16),
        grid=(seqs, heads // together),
        in_specs=[
            per_head,
            pl.BlockSpec((old.shape[0], 1) + old.shape[2:], lambda s, h: (0, s, 0, 0, 0)),
            per_seq,
            per_seq,
            per_seq,
            per_seq,
            pl.BlockSpec((1, 1, bias.shape[2]), lambda s, h: (s, 0, 0)),
        ],
        out_specs=per_head,
        scratch_shapes=[pltpu.VMEM((NEW, HD), jnp.bfloat16)],
        compiler_params=pltpu.CompilerParams(vmem_limit_bytes=48 * 2**20),
        name="attention",
    )(query, old, key_raw, value, cosine, sine, bias)


def output_phases(
    order, greet, mixture, weight, destination, result,
    everyone, weight_all, incoming,
    weight_sem, send_sem, recv_sem, swap_send, swap_recv,
):
    position, index = order
    n = incoming.shape[0]
    half, part = incoming.shape[3], incoming.shape[4]
    width = 2 * part
    me = lax.axis_index("tensor")
    worker = lax.axis_index("worker")
    workers = everyone.shape[0]
    place = position(me)
    forward = index(lax.rem(place + 1, n))
    back = index(lax.rem(place + n - 1, n))
    targets = (forward, back)

    def weight_copy(block):
        cols = pl.ds(pl.multiple_of(block * width, width), width)
        return pltpu.make_async_copy(
            weight.at[:, cols], weight_all.at[block], weight_sem.at[block]
        )

    def start_weights(k, carry):
        weight_copy(index(lax.rem(place + n - 1 - k, n))).start()

        @pl.when(k < n // 2 - 1)
        def _():
            weight_copy(index(lax.rem(place + 1 + k, n))).start()

        return carry

    def begin():
        if greet:
            barrier = pltpu.get_barrier_semaphore()
            for target in targets:
                pl.semaphore_signal(
                    barrier, inc=1, device_id={"tensor": target}, device_id_type=MESH
                )
            for k in range(1, workers):
                pl.semaphore_signal(
                    barrier,
                    inc=1,
                    device_id={"worker": lax.rem(worker + k, workers)},
                    device_id_type=MESH,
                )
        lax.fori_loop(0, n // 2, start_weights, 0)
        weight_copy(me).start()
        for r in range(2):
            for d in range(2):
                incoming[0, r, d] = jnp.zeros((half, part), jnp.bfloat16)
        if greet:
            pl.semaphore_wait(barrier, 1 + workers)

    def hop(step, r, d):
        return pltpu.make_async_remote_copy(
            src_ref=incoming.at[step, r, d],
            dst_ref=incoming.at[step + 1, r, d],
            send_sem=send_sem.at[step, r, d],
            recv_sem=recv_sem.at[step + 1, r, d],
            device_id={"tensor": targets[d]},
            device_id_type=MESH,
        )

    def arrival(step, r, d):
        return pltpu.make_async_remote_copy(
            src_ref=incoming.at[step, r, d],
            dst_ref=incoming.at[step, r, d],
            send_sem=send_sem.at[step, r, d],
            recv_sem=recv_sem.at[step, r, d],
            device_id={"tensor": targets[d]},
            device_id_type=MESH,
        )

    def add_up(step, r):
        blocks = (
            index(lax.rem(place + 2 * n - 1 - step, n)),
            index(lax.rem(place + 1 + step, n)),
        )

        if r == 0:

            @pl.when(step < n // 2)
            def _():
                weight_copy(blocks[0]).wait()

            @pl.when(step < n // 2 - 1)
            def _():
                weight_copy(blocks[1]).wait()

            @pl.when(step == n // 2)
            def _():
                weight_copy(me).wait()

        for d in range(2):
            product = jnp.dot(
                mixture[r * half : (r + 1) * half, :],
                weight_all[blocks[d], :, d * part : (d + 1) * part],
                preferred_element_type=jnp.float32,
            )

            @pl.when(step > 0)
            def _():
                arrival(step, r, d).wait_recv()

            summed = product + incoming[step, r, d].astype(jnp.float32)
            incoming[step, r, d] = summed.astype(jnp.bfloat16)

            @pl.when(step < n - 1)
            def _():
                hop(step, r, d).start()

    def swap(k, r):
        return pltpu.make_async_remote_copy(
            src_ref=everyone.at[worker, pl.ds(r * half, half)],
            dst_ref=everyone.at[worker, pl.ds(r * half, half)],
            send_sem=swap_send.at[k, r],
            recv_sem=swap_recv.at[k, r],
            device_id={"worker": lax.rem(worker + k, workers)},
            device_id_type=MESH,
        )

    def hand_over(r):
        for d in range(2):
            everyone[worker, r * half : (r + 1) * half, d * part : (d + 1) * part] = incoming[
                n - 1, r, d
            ]
        for k in range(1, workers):
            swap(k, r).start()

    def sums():
        def step_body(step, carry):
            add_up(step + 1, 0)
            add_up(step, 1)
            return carry

        lax.fori_loop(0, n - 1, step_body, 0)
        hand_over(0)
        add_up(n - 1, 1)
        hand_over(1)

    def end():
        def finish(step, carry):
            for r in range(2):
                for d in range(2):
                    hop(step, r, d).wait_send()
            return carry

        lax.fori_loop(0, n - 1, finish, 0)
        for r in range(2):
            for k in range(1, workers):
                swap(k, r).wait()

        seqs = destination.shape[0]
        local_seqs = seqs // workers
        bound = [jnp.where(destination[seq] == worker, 1, 0) for seq in range(seqs)]
        rank, ranks = 0, []
        for seq in range(seqs):
            ranks.append(rank)
            rank = rank + bound[seq]
        for slot in range(result.shape[0]):
            chosen = [jnp.where(ranks[seq] == slot, bound[seq], 0) for seq in range(seqs)]
            picked = jnp.zeros(result.shape[1:], result.dtype)
            for seq in range(seqs):
                first = seq % local_seqs * NEW
                rows = everyone[seq // local_seqs, first : first + NEW, :]
                flag = jnp.full(result.shape[1:], chosen[seq], jnp.int32)
                picked = jnp.where(flag > 0, rows, picked)
            result[slot] = picked

    return begin, add_up, sums, end


def output_kernel(order, *refs):
    begin, add_up, sums, end = output_phases(order, True, *refs)
    begin()
    add_up(0, 0)
    sums()
    end()


def output_scratch(n, workers, rows, depth, width):
    half, part = rows // 2, width // 2
    return [
        pltpu.VMEM((workers, rows, width), jnp.bfloat16),
        pltpu.VMEM((n, depth, width), jnp.bfloat16),
        pltpu.VMEM((n, 2, 2, half, part), jnp.bfloat16),
        pltpu.SemaphoreType.DMA((n,)),
        pltpu.SemaphoreType.DMA((n, 2, 2)),
        pltpu.SemaphoreType.DMA((n, 2, 2)),
        pltpu.SemaphoreType.DMA((workers, 2)),
        pltpu.SemaphoreType.DMA((workers, 2)),
    ]


def project_out(order, n, workers, mixture, weight, destination):
    rows, depth = mixture.shape
    width = weight.shape[1] // n
    vmem = pl.BlockSpec(memory_space=pltpu.VMEM)
    return pl.pallas_call(
        functools.partial(output_kernel, order),
        out_shape=jax.ShapeDtypeStruct((CAP, NEW, width), jnp.bfloat16),
        in_specs=[
            vmem,
            pl.BlockSpec(memory_space=pl.ANY),
            pl.BlockSpec(memory_space=pltpu.SMEM),
        ],
        out_specs=vmem,
        scratch_shapes=output_scratch(n, workers, rows, depth, width),
        compiler_params=pltpu.CompilerParams(
            collective_id=1, has_side_effects=True, vmem_limit_bytes=48 * 2**20
        ),
        name="project_out",
    )(mixture, weight, destination)


def layer_kernel(
    order, grid, seqs, scratch_counts,
    tok, gain, inverse, lengths, wq, wk, wv, cached, tables, weight, destination, result,
    seen, query, key_raw, value, cosine, sine, ctx, mixture, *scratch,
):
    first = scratch_counts
    begin, add_up, sums, end = output_phases(
        order, False, mixture, weight, destination, result, *scratch[first:]
    )
    project_kernel(
        grid, seqs, True, begin, tok, gain, inverse, lengths, wq, wk, wv, cached,
        query, key_raw, value, cosine, sine, ctx, *scratch[:first],
    )
    worker = lax.axis_index("worker")
    count = ctx.shape[0] * ctx.shape[3]
    heads = query.shape[1] // HD
    together = math.gcd(heads, 4)

    def look(seq):
        row = tables[pl.ds(worker * seqs + seq, 1), :].astype(jnp.float32)
        rows = jnp.broadcast_to(row, (8, row.shape[1])).astype(jnp.bfloat16)
        slot = lax.broadcasted_iota(jnp.int32, (row.shape[1], count), 1)
        block = lax.broadcasted_iota(jnp.int32, (row.shape[1], count), 0)
        pick = jnp.where(lax.div(slot, BLK) == block, 1.0, 0.0).astype(jnp.bfloat16)
        held = jnp.dot(rows, pick, preferred_element_type=jnp.float32)
        inside = lax.broadcasted_iota(jnp.int32, held.shape, 1)
        logical = held.astype(jnp.int32) * BLK + lax.rem(inside, BLK)
        return jnp.where(logical < lengths[worker * seqs + seq], 1.0, 0.0)

    def attend(seq):
        seen[...] = look(seq)
        lines = slice(seq * NEW, (seq + 1) * NEW)
        raw = key_raw[lines, :].astype(jnp.float32)
        turned = pltpu.roll(raw, HD // 2, 1)
        key = (raw * cosine[lines, :] + turned * sine[lines, :]).astype(jnp.bfloat16)
        key_raw[lines, :] = key

        def some(number, carry):
            attend_heads(
                query,
                ctx[:, seq, 0].reshape(count, HD),
                ctx[:, seq, 1].reshape(count, HD),
                key_raw[lines, :],
                value[lines, :],
                seen[0:1, :] > 0,
                mixture,
                [
                    pl.ds(pl.multiple_of((number * together + k) * HD, HD), HD)
                    for k in range(together)
                ],
                lines,
            )
            return carry

        lax.fori_loop(0, heads // together, some, 0)

    for seq in range(seqs // 2):
        attend(seq)
    add_up(0, 0)
    for seq in range(seqs // 2, seqs):
        attend(seq)
    sums()
    end()


def layer(order, grid, n, workers, tokens, gain, inverse, lengths, wq, wk, wv, cached, tables, weight, destination):
    rows = tokens.shape[0]
    cols, narrow = wq.shape[1], wk.shape[1]
    width = weight.shape[1] // n
    seqs, stored = cached.shape[0], cached.shape[1]
    vmem = pl.BlockSpec(memory_space=pltpu.VMEM)
    smem = pl.BlockSpec(memory_space=pltpu.SMEM)
    anywhere = pl.BlockSpec(memory_space=pl.ANY)
    scratch = project_scratch(grid, n, tokens, gain, wq, wk, cached)
    return pl.pallas_call(
        functools.partial(layer_kernel, order, grid, seqs, len(scratch)),
        out_shape=jax.ShapeDtypeStruct((CAP, NEW, width), jnp.bfloat16),
        in_specs=[anywhere, anywhere, vmem, smem] + [anywhere] * 4 + [vmem, anywhere, smem],
        out_specs=vmem,
        scratch_shapes=[
            pltpu.VMEM((8, n * stored), jnp.float32),
            pltpu.VMEM((rows, cols), jnp.bfloat16),
            pltpu.VMEM((rows, narrow), jnp.bfloat16),
            pltpu.VMEM((rows, narrow), jnp.bfloat16),
            pltpu.VMEM((rows, HD), jnp.float32),
            pltpu.VMEM((rows, HD), jnp.float32),
            pltpu.VMEM((n, seqs, 2, stored, HD), jnp.bfloat16),
            pltpu.VMEM((rows, cols), jnp.bfloat16),
        ]
        + scratch
        + output_scratch(n, workers, rows, cols, width),
        compiler_params=pltpu.CompilerParams(
            collective_id=2, has_side_effects=True, vmem_limit_bytes=57 * 2**20
        ),
        name="layer",
    )(tokens, gain, inverse, lengths, wq, wk, wv, cached, tables, weight, destination)


def from_partner(block, axis, bit):
    count = lax.axis_size(axis)
    route = []
    for low in range(count):
        high = low | 1 << bit
        if high != low and high < count:
            route += [(low, high), (high, low)]
    return lax.ppermute(block, axis, route)


def whole_head(block, bits):
    me = lax.axis_index("tensor")
    for bit in range(bits):
        other = from_partner(block, "tensor", bit)
        upper = me // (1 << bit) % 2 == 1
        block = jnp.where(
            upper,
            jnp.concatenate([other, block], axis=1),
            jnp.concatenate([block, other], axis=1),
        )
    return block


def local(
    ring,
    grid,
    tokens,
    norm_gain,
    query_weight,
    key_weight,
    value_weight,
    output_weight,
    cached_blocks,
    cache_length,
    block_table,
    destination,
):
    n = lax.axis_size("tensor")
    workers = lax.axis_size("worker")
    seqs = cached_blocks.shape[0]
    logical = block_table[:, :, None] * BLK + jnp.arange(BLK, dtype=jnp.int32)[None, None, :]
    seen = (logical < cache_length[:, None, None]).astype(jnp.float32)
    seen = seen.reshape(cache_length.shape[0], 1, -1)
    half = 500000.0 ** (-(np.arange(HD // 2) * 2.0 / HD))
    inverse = jnp.asarray(np.concatenate([half, half])[None, :], jnp.float32)
    gain = norm_gain[None, :]
    bits = (n // KVH).bit_length() - 1
    if bits == 0:
        return layer(
            ring, grid, n, workers, tokens, gain, inverse, cache_length,
            query_weight, key_weight, value_weight, cached_blocks, block_table,
            output_weight, destination,
        )[None]
    query, key_raw, value, cosine, sine, old = project(
        grid, n, tokens, gain, inverse, cache_length,
        query_weight, key_weight, value_weight, cached_blocks,
    )
    key_raw, value = whole_head(key_raw, bits), whole_head(value, bits)
    seen = lax.dynamic_slice_in_dim(seen, lax.axis_index("worker") * seqs, seqs, 0)
    mixture = attention(query, old, key_raw, value, cosine, sine, seen)
    return project_out(ring, n, workers, mixture, output_weight, destination)[None]


def solution(mesh):
    placed = (
        P(("groups", "worker"), "tensor"),
        P(),
        P(None, "tensor"),
        P(None, "tensor"),
        P(None, "tensor"),
        P("tensor", None),
        P(("groups", "worker"), "tensor", None, None),
        P("groups"),
        P("groups", None),
        P("groups"),
    )
    return jax.shard_map(
        functools.partial(local, *layout(mesh)),
        mesh=mesh,
        in_specs=placed,
        out_specs=P(("groups", "worker"), None, None, "tensor"),
        check_vma=False,
    )
```
